128 devices in a mesh: win: 2 (over x_hi), seq: 16 (over y, x_lo, core), head: 4 (over z).
Axes of the slice: x: 4 (x_hi: 2, x_lo: 2; x = x_hi * 2 + x_lo), y: 4, z: 4, core: 2. Of those that a mesh axis runs over, the one named last changes fastest.
Arguments:
- queries: bfloat16 [8192, 3072], P(('win', 'seq'), 'head'), parts along dimension 0, may hold values from -28 to 28
- keys_in: bfloat16 [8192, 3072], P(('win', 'seq'), 'head'), parts along dimension 0, may hold values from -28 to 28
- values_in: bfloat16 [8192, 3072], P(('win', 'seq'), 'head'), parts along dimension 0, may hold values from -6 to 6
- forward_out: bfloat16 [8192, 3072], P(('win', 'seq'), 'head'), parts along dimension 0, may hold values from -6 to 6
- grad_out: bfloat16 [8192, 3072], P(('win', 'seq'), 'head'), parts along dimension 0, may hold values from -6 to 6
- lengths: int32 [16], P('win'), parts along dimension 0, may hold values from 1 to 2048, 4096 in all
- query_block: int32 [64], P(('win', 'seq')), parts along dimension 0, may hold values from 0 to 31, each once
Outputs:
- grad_query: bfloat16 [8192, 3072], P(('win', 'seq'), 'head'), parts along dimension 0
- grad_key: bfloat16 [8192, 3072], P(('win', 'seq'), 'head'), parts along dimension 0
- grad_value: bfloat16 [8192, 3072], P(('win', 'seq'), 'head'), parts along dimension 0
The draws below stay inside these ranges and needn't reach their ends.
There are 2 independent parts, one for each index of `win`. The reference program is written for one: setup_inputs(seed, part) draws one part's arguments, and reference() takes and returns one part's arrays. A program takes and returns all parts, laid end to end along the dimension named above; each array names one. Nothing has to cross between parts.
Inputs may be any that keep to these rules, and one draw needn't show every extreme that they name: `lengths`: whole numbers that sum to 4096; the largest is exactly 2048. `query_block`: each number once.
All inputs are finite; a program needn't handle non-finite values.
Results may differ from the reference program's by a relative error of at most 0.0051.
Values may be sent and summed in bfloat16 or wider, within the bound.
No kernel may reach another device: no remote copies, remote signals or barrier semaphores. Data moves between devices by JAX's collectives and lax.ppermute only.
A program may use at most 128 MiB of HBM per device.

```python
import math
import jax
import jax.numpy as jnp
import numpy as np
from jax import lax

HEADS = 24
HD = 128
QBLK = 128
VIDS = 8
TOKENS = 4096
QBLOCKS = 32


def draw_queries(key, part):
    key = jax.random.fold_in(key, 11)
    noise_key = jax.random.fold_in(key, 0)
    noise = jnp.clip(jax.random.normal(noise_key, (TOKENS, HEADS * HD), jnp.float32), -6.0, 6.0)
    return noise.astype(jnp.bfloat16)


def draw_keys_in(key, part):
    key = jax.random.fold_in(key, 23)
    noise_key = jax.random.fold_in(key, 0)
    noise = jnp.clip(jax.random.normal(noise_key, (TOKENS, HEADS * HD), jnp.float32), -6.0, 6.0)
    return noise.astype(jnp.bfloat16)


def block_levels(stream_key, shape, pieces, least, high):
    def one(position, shards_of):
        draws = jax.random.uniform(jax.random.fold_in(jax.random.fold_in(stream_key, 6), position), (shards_of,), jnp.float32, least / len(pieces), high / len(pieces))
        return jnp.repeat(jnp.exp(draws), shape[position] // shards_of).reshape((-1,) + (1,) * (len(shape) - position - 1))

    factor_of = one(*pieces[0])
    for cut in pieces[1:]:
        factor_of = factor_of * one(*cut)
    return factor_of


def split_up(number_of, total, bound, lean):
    portions = [(1 << 20) // math.isqrt(grade ** lean) + 1 for grade in range(2, number_of + 1)]
    rest, counts = total - bound - (number_of - 1), [1] * (number_of - 1)
    while rest > 0:
        candidates = [i for i in range(number_of - 1) if counts[i] < bound]
        whole, remaining = sum([portions[i] for i in candidates]), rest
        for i in candidates:
            extra = min(bound - counts[i], max(1, remaining * portions[i] // whole), rest)
            counts[i] = counts[i] + extra
            rest = rest - extra
    return np.array([bound] + counts)


def ragged(stream_key, number_of, total, limit, skew):
    if number_of == 2:
        one = jax.random.randint(stream_key, (), max(1, total - limit), min(limit, total - 1) + 1)
        return jnp.stack([one, total - one])
    tallies = jnp.asarray(split_up(number_of, total, limit, skew), jnp.int32)
    couples = (number_of - 1) // 2
    donor, receiver = tallies[1:1 + 2 * couples:2], tallies[2:2 + 2 * couples:2]
    margin = jnp.minimum(donor - 1, limit - receiver)
    moved = jax.random.randint(jax.random.fold_in(stream_key, 1), (couples,), 0, 1 << 20) % (margin + 1)
    tallies = tallies.at[1:1 + 2 * couples:2].set(donor - moved).at[2:2 + 2 * couples:2].set(receiver + moved)
    return tallies[jax.random.permutation(jax.random.fold_in(stream_key, 2), number_of)]


def gaussian(stream_key, dims, spread, reach, cuts=(), kind=jnp.bfloat16):
    entries = jax.random.normal(stream_key, dims, jnp.float32) * spread
    if len(cuts) > 0:
        entries = block_levels(stream_key, dims, cuts, -0.22, 0.18) * entries
    return jnp.clip(entries, min=-reach, max=reach).astype(kind)


def setup_inputs(seed: int = 0, part: int = 0) -> dict:
    streams_of = jax.random.split(jax.random.key(seed), 8)
    own_keys = jax.random.split(jax.random.fold_in(streams_of[7], part), 8)
    return {
        "queries": draw_queries(jax.random.fold_in(jax.random.fold_in(streams_of[7], part), 71), part),
        "keys_in": draw_keys_in(jax.random.fold_in(jax.random.fold_in(streams_of[7], part), 71), part),
        "values_in": gaussian(own_keys[2], (TOKENS, HEADS * HD), 1.0, 6.0, ((0, 16), (1, 4))),
        "forward_out": gaussian(own_keys[3], (TOKENS, HEADS * HD), 1.0, 6.0, ((0, 16), (1, 4))),
        "grad_out": gaussian(own_keys[4], (TOKENS, HEADS * HD), 1.0, 6.0, ((0, 16), (1, 4))),
        "lengths": ragged(own_keys[5], VIDS, TOKENS, TOKENS // 2, 2).astype(jnp.int32),
        "query_block": jax.random.permutation(own_keys[6], QBLOCKS).astype(jnp.int32),
    }


def doc_index(positions, offsets):
    return jnp.sum((positions[:, None] >= offsets[None, :]).astype(jnp.int32), axis=1).astype(jnp.int32) - 1


def heads_first(array):
    return array.reshape(TOKENS, HEADS, HD).transpose(1, 0, 2)


def heads_last(array):
    return array.transpose(1, 0, 2).reshape(TOKENS, HEADS * HD)


def reference(queries, keys_in, values_in, forward_out, grad_out, lengths, query_block):
    scale_factor = HD ** -0.5
    offsets = (jnp.cumsum(lengths) - lengths).astype(jnp.int32)
    positions = jnp.arange(TOKENS, dtype=jnp.int32)
    query_tokens = (query_block[:, None] * QBLK + jnp.arange(QBLK, dtype=jnp.int32)[None, :]).reshape(TOKENS)
    query_docs = doc_index(query_tokens, offsets)
    key_docs = doc_index(positions, offsets)
    allowed = query_docs[:, None] == key_docs[None, :]

    def one_head(items):
        query_h, key_h, value_h, out_h, grad_h = items
        scores = jnp.dot(query_h, key_h.T, preferred_element_type=jnp.float32) * scale_factor
        top = jnp.max(jnp.where(allowed, scores, -jnp.inf), axis=1, keepdims=True)
        total = jnp.sum(jnp.where(allowed, jnp.exp(scores - top), 0.0), axis=1, keepdims=True)
        lse = top + jnp.log(total)
        probs = jnp.where(allowed, jnp.exp(scores - lse), 0.0)
        grad_value = jnp.dot(probs.astype(jnp.bfloat16).T, grad_h, preferred_element_type=jnp.float32)
        grad_probs = jnp.dot(grad_h, value_h.T, preferred_element_type=jnp.float32)
        delta = jnp.sum(grad_h.astype(jnp.float32) * out_h.astype(jnp.float32), axis=1, keepdims=True)
        grad_scores = (probs * (grad_probs - delta)).astype(jnp.bfloat16)
        grad_query = jnp.dot(grad_scores, key_h, preferred_element_type=jnp.float32) * scale_factor
        grad_key = jnp.dot(grad_scores.T, query_h, preferred_element_type=jnp.float32) * scale_factor
        return grad_query.astype(jnp.bfloat16), grad_key.astype(jnp.bfloat16), grad_value.astype(jnp.bfloat16)

    grad_query, grad_key, grad_value = lax.map(one_head, (heads_first(queries), heads_first(keys_in), heads_first(values_in), heads_first(forward_out), heads_first(grad_out)))
    return heads_last(grad_query), heads_last(grad_key), heads_last(grad_value)
```

```python
import functools
import math

import jax
import jax.numpy as jnp
from jax import lax
from jax.experimental import pallas as pl
from jax.experimental.pallas import tpu as pltpu
from jax.sharding import PartitionSpec as P

HD = 128
QBLK = 128
CHUNK = 256
TILE = 2 * QBLK
SCALE = HD ** (-0.5)
RATE = SCALE * math.log2(math.e)
FLOOR = -1e30
EXTRA = 16


def dot_nt(a, b):
    return lax.dot_general(a, b, (((1,), (1,)), ((), ())), preferred_element_type=jnp.float32)


def dot_nn(a, b):
    return lax.dot_general(a, b, (((1,), (0,)), ((), ())), preferred_element_type=jnp.float32)


def dot_tn(a, b):
    return lax.dot_general(a, b, (((0,), (0,)), ((), ())), preferred_element_type=jnp.float32)


def head_kernel(
    core_ref, order_ref, count_ref, list_ref,
    qd_ref, kv_own, kv_other, low_ref, high_ref,
    dq_ref, keep_ref, send_ref,
    keys, values, qs, gs, scores, probs, grads, acc_k, acc_v, acc_q,
):
    core = core_ref[0]
    chips = kv_own.shape[0]
    tiles = low_ref.shape[0]

    def place(i, carry):
        mine, theirs = 2 * i + core, 2 * i + 1 - core
        keys[mine] = kv_own[i, 0]
        values[mine] = kv_own[i, 1]
        keys[theirs] = kv_other[i, 0]
        values[theirs] = kv_other[i, 1]
        zero = jnp.zeros((CHUNK, HD), jnp.float32)
        for spot in (mine, theirs):
            acc_k[spot] = zero
            acc_v[spot] = zero
        return carry

    lax.fori_loop(0, chips, place, 0)

    def tile(t, carry):
        a, b = order_ref[2 * t], order_ref[2 * t + 1]
        count = count_ref[t]
        deltas = []
        for slot, block in ((0, a), (1, b)):
            chip, half = block // 2, block % 2
            at = pl.multiple_of(half * QBLK, QBLK)
            rows = pl.ds(slot * QBLK, QBLK)
            qs[rows, :] = qd_ref[chip, pl.ds(at, QBLK), :]
            gs[rows, :] = qd_ref[chip, pl.ds(CHUNK + at, QBLK), :]
            parts = qd_ref[chip, 2 * CHUNK : 2 * CHUNK + EXTRA, :].astype(jnp.float32)
            both = [parts[r : r + 1] + parts[r + 2 : r + 3] + parts[r + 4 : r + 5] for r in (0, 1)]
            deltas.append(jnp.where(half == 0, both[0], both[1]))
        delta = jnp.concatenate(deltas, axis=1)
        low = low_ref[t]
        span = high_ref[t] - low

        scores[0] = dot_nt(keys[list_ref[t, 0]], qs[...])

        def totals(i, carry):
            top, total = carry
            spot = list_ref[t, i]
            after = list_ref[t, jnp.minimum(i + 1, count - 1)]
            scores[i + 1] = dot_nt(keys[after], qs[...])
            position = spot * CHUNK + lax.broadcasted_iota(jnp.int32, (CHUNK, TILE), 0) - low
            allowed = (position >= 0) & (position < span)
            s = jnp.where(allowed, scores[i], FLOOR)
            scores[i] = s
            s = s.reshape(CHUNK // 8, 8, TILE)
            new_top = jnp.maximum(top, jnp.max(s, axis=0))
            added = jnp.sum(jnp.exp2((s - new_top[None]) * RATE), axis=0)
            return new_top, total * jnp.exp2((top - new_top) * RATE) + added

        top, total = lax.fori_loop(
            0, count, totals,
            (jnp.full((8, TILE), FLOOR, jnp.float32), jnp.zeros((8, TILE), jnp.float32)),
        )
        row_top = jnp.max(top, axis=0, keepdims=True)
        row_sum = jnp.sum(total * jnp.exp2((top - row_top) * RATE), axis=0, keepdims=True)
        level = row_top + jnp.log2(row_sum) * (1.0 / RATE)

        acc_q[...] = jnp.zeros_like(acc_q)

        def first_half(i):
            spot = list_ref[t, jnp.minimum(i, count - 1)]
            p = jnp.exp2((scores[i] - level) * RATE)
            dp = dot_nt(values[spot], gs[...])
            probs[i % 2] = p.astype(jnp.bfloat16)
            grads[i % 2] = (p * (dp - delta)).astype(jnp.bfloat16)

        def second_half(i):
            spot = list_ref[t, i]
            pb = probs[i % 2]
            sb = grads[i % 2]
            acc_v[spot] += dot_nn(pb, gs[...])
            acc_k[spot] += dot_nn(sb, qs[...])
            acc_q[...] += dot_tn(sb, keys[spot])

        first_half(0)

        def turn(i, carry):
            first_half(i + 1)
            second_half(i)
            return carry

        lax.fori_loop(0, count, turn, 0)
        result = (acc_q[...] * SCALE).astype(jnp.bfloat16)
        dq_ref[a] = result[:QBLK]
        dq_ref[b] = result[QBLK:]
        return carry

    lax.fori_loop(0, tiles, tile, 0)

    def hand_out(i, carry):
        mine, theirs = 2 * i + core, 2 * i + 1 - core
        keep_ref[i, 0] = acc_k[mine] * SCALE
        keep_ref[i, 1] = acc_v[mine]
        send_ref[i, 0] = (acc_k[theirs] * SCALE).astype(jnp.bfloat16)
        send_ref[i, 1] = acc_v[theirs].astype(jnp.bfloat16)
        return carry

    lax.fori_loop(0, chips, hand_out, 0)


def head_grads(core, order, count, chunk_list, qd, kv_own, kv_other, low, high):
    chips = kv_own.shape[0]
    blocks = 2 * chips
    smem = pl.BlockSpec(memory_space=pltpu.SMEM)
    vmem = pl.BlockSpec(memory_space=pltpu.VMEM)
    pairs = blocks * QBLK * 2048
    return pl.pallas_call(
        head_kernel,
        out_shape=(
            jax.ShapeDtypeStruct((blocks, QBLK, HD), jnp.bfloat16),
            jax.ShapeDtypeStruct((chips, 2, CHUNK, HD), jnp.float32),
            jax.ShapeDtypeStruct((chips, 2, CHUNK, HD), jnp.bfloat16),
        ),
        in_specs=[smem] * 4 + [vmem] * 5,
        out_specs=(vmem,) * 3,
        scratch_shapes=[
            pltpu.VMEM((blocks, CHUNK, HD), jnp.bfloat16),
            pltpu.VMEM((blocks, CHUNK, HD), jnp.bfloat16),
            pltpu.VMEM((TILE, HD), jnp.bfloat16),
            pltpu.VMEM((TILE, HD), jnp.bfloat16),
            pltpu.VMEM((blocks + 1, CHUNK, TILE), jnp.float32),
            pltpu.VMEM((2, CHUNK, TILE), jnp.bfloat16),
            pltpu.VMEM((2, CHUNK, TILE), jnp.bfloat16),
            pltpu.VMEM((blocks, CHUNK, HD), jnp.float32),
            pltpu.VMEM((blocks, CHUNK, HD), jnp.float32),
            pltpu.VMEM((TILE, HD), jnp.float32),
        ],
        compiler_params=pltpu.CompilerParams(vmem_limit_bytes=40 * 1024 * 1024),
        cost_estimate=pl.CostEstimate(
            flops=12 * pairs * HD, bytes_accessed=8 * 2**20, transcendentals=2 * pairs
        ),
    )(core, order, count, chunk_list, qd, kv_own, kv_other, low, high)


def plan(ids, lengths):
    blocks = ids.shape[0]
    ends = jnp.cumsum(lengths)
    offsets = ends - lengths
    place = jnp.arange(blocks, dtype=jnp.int32)
    rank = jnp.sum((ids[None, :] < ids[:, None]).astype(jnp.int32), axis=1)
    hit = (rank[None, :] == place[:, None]).astype(jnp.int32)
    order = jnp.sum(hit * place[None, :], axis=1)
    sorted_ids = jnp.sum(hit * ids[None, :], axis=1)
    tokens = sorted_ids[:, None] * QBLK + jnp.arange(QBLK, dtype=jnp.int32)[None, :]
    inside = (tokens[..., None] >= offsets) & (tokens[..., None] < ends)
    low = jnp.sum(jnp.where(inside, offsets, 0), axis=-1)
    high = jnp.sum(jnp.where(inside, ends, 0), axis=-1)
    first = low[:, 0] // CHUNK
    last = (high[:, QBLK - 1] - 1) // CHUNK
    needed = (place[None, :] >= first[:, None]) & (place[None, :] <= last[:, None])
    needed = (needed[0::2] | needed[1::2]).astype(jnp.int32)
    count = jnp.sum(needed, axis=1)
    before = jnp.cumsum(needed, axis=1) - needed
    chosen = (before[:, None, :] == place[None, :, None]) & (needed[:, None, :] > 0)
    chunk_list = jnp.sum(jnp.where(chosen, place[None, None, :], 0), axis=2)
    shape = (blocks // 2, 1, TILE)
    return order, count, chunk_list, low.reshape(shape), high.reshape(shape)


def split_in_three(x):
    parts = []
    for _ in range(3):
        part = lax.reduce_precision(x, exponent_bits=8, mantissa_bits=7)
        parts.append(part.astype(jnp.bfloat16))
        x = x - part
    return parts


def on_device(queries, keys_in, values_in, forward_out, grad_out, lengths, query_block):
    size = lax.axis_size("seq")
    chips = size // 2
    core = lax.axis_index("seq") % 2
    rows = queries.shape[0]
    heads = queries.shape[1] // HD
    groups = [[2 * i + c for i in range(chips)] for c in range(2)]
    swap = [(i, i ^ 1) for i in range(size)]

    def by_head(x):
        return x.reshape(rows, heads, HD).transpose(1, 0, 2)

    def padded(x):
        return jnp.pad(x, ((0, chips - heads),) + ((0, 0),) * (x.ndim - 1))

    def exchange(x):
        return lax.all_to_all(x, "seq", 0, 0, axis_index_groups=groups)

    ids = lax.all_gather(query_block, "seq", axis=0, tiled=True).reshape(chips, 2, 2)
    ids = lax.dynamic_index_in_dim(ids, core, 1, keepdims=False).reshape(2 * chips)
    order, count, chunk_list, low, high = plan(ids, lengths)

    kv = padded(jnp.stack([by_head(keys_in), by_head(values_in)], axis=1))
    kv_own = exchange(kv)
    kv_other = lax.ppermute(kv_own, "seq", swap)

    delta = jnp.sum(
        (grad_out.astype(jnp.float32) * forward_out.astype(jnp.float32)).reshape(rows, heads, HD),
        axis=2,
    )
    delta = delta.T.reshape(heads, rows // QBLK, QBLK)
    extra = jnp.concatenate(split_in_three(delta), axis=1)
    extra = jnp.pad(extra, ((0, 0), (0, EXTRA - extra.shape[1]), (0, 0)))
    qd = padded(jnp.concatenate([by_head(queries), by_head(grad_out), extra], axis=1))
    qd = exchange(qd)

    core_arg = jnp.full((1,), core, jnp.int32)
    dq, keep, send = head_grads(core_arg, order, count, chunk_list, qd, kv_own, kv_other, low, high)
    dq = exchange(dq.reshape(chips, rows, HD))
    received = lax.ppermute(send, "seq", swap)
    dkv = (keep + received.astype(jnp.float32)).astype(jnp.bfloat16)
    dkv = exchange(dkv)

    def by_row(x):
        return x[:heads].transpose(1, 0, 2).reshape(rows, heads * HD)

    return by_row(dq), by_row(dkv[:, 0]), by_row(dkv[:, 1])


def solution(mesh):
    spec = P(("win", "seq"), "head")
    in_specs = (spec,) * 5 + (P("win"), P(("win", "seq")))
    return jax.shard_map(
        on_device, mesh=mesh, in_specs=in_specs, out_specs=(spec,) * 3, check_vma=False
    )
```

```python
import math

import jax
import jax.numpy as jnp
from jax import lax
from jax.experimental import pallas as pl
from jax.experimental.pallas import tpu as pltpu
from jax.sharding import PartitionSpec as P

HD = 128
QBLK = 128
CHUNK = 256
TILE = 2 * QBLK
GROUP = 3
SCALE = HD ** (-0.5)
RATE = SCALE * math.log2(math.e)
FLOOR = -1e30
EXTRA = 16

smem = pl.BlockSpec(memory_space=pltpu.SMEM)
vmem = pl.BlockSpec(memory_space=pltpu.VMEM)
params = pltpu.CompilerParams(vmem_limit_bytes=40 * 1024 * 1024)


def dot(a, b):
    return jnp.dot(a, b, preferred_element_type=jnp.float32)


def pack_kernel(ids_ref, k_ref, v_ref, q_ref, out_ref):
    rows = k_ref.shape[0]
    heads = k_ref.shape[1] // HD
    for slot in range(out_ref.shape[0]):
        for i, ref in enumerate((k_ref, v_ref, q_ref)):
            at = slice(i * rows, (i + 1) * rows)
            if slot < heads:
                out_ref[slot, at, :] = ref[:, slot * HD : (slot + 1) * HD]
            else:
                out_ref[slot, at, :] = jnp.zeros((rows, HD), out_ref.dtype)
        out_ref[slot, 3 * rows :, :] = ids_ref[...]


def pack(ids, k, v, q, chips):
    rows = k.shape[0]
    return pl.pallas_call(
        pack_kernel,
        out_shape=jax.ShapeDtypeStruct((chips, 3 * rows + EXTRA, HD), k.dtype),
        in_specs=[vmem] * 4,
        out_specs=vmem,
        name="pack",
    )(ids, k, v, q)


def prepare_kernel(
    core_ref, order_ref, count_ref, list_ref, first_ref, other_ref, key_code, query_code,
    keys, keys_t, values, qs, qt, level_ref, raw,
):
    core = core_ref[0]
    chips = first_ref.shape[0]
    tiles = query_code.shape[0]

    def place(i, carry):
        mine, theirs = 2 * i + core, 2 * i + 1 - core
        for spot, ref in ((mine, first_ref), (theirs, other_ref)):
            k = ref[i, :CHUNK, :]
            keys[spot, :, :HD] = k
            keys[spot, :, HD:] = key_code[spot]
            keys_t[spot] = k.T
            values[spot, :, :HD] = ref[i, CHUNK : 2 * CHUNK, :]
            values[spot, :, HD:] = jnp.full((CHUNK, HD), -1, jnp.bfloat16)
        return carry

    lax.fori_loop(0, chips, place, 0)
    keys[2 * chips] = jnp.ones((CHUNK, 2 * HD), jnp.bfloat16)

    def tile(t, carry):
        for slot in range(2):
            block = order_ref[2 * t + slot]
            at = pl.multiple_of(2 * CHUNK + block % 2 * QBLK, QBLK)
            q = first_ref[block // 2, pl.ds(at, QBLK), :]
            rows = slice(slot * QBLK, (slot + 1) * QBLK)
            qs[t, rows, :] = q
            qt[t, :HD, rows] = q.T
        qt[t, HD:, :] = query_code[t].T
        steps = (count_ref[t] + GROUP - 1) // GROUP

        def score(i):
            i = jnp.minimum(i, steps - 1)
            for u in range(GROUP):
                raw[i % 2, u] = dot(keys[list_ref[t, GROUP * i + u]], qt[t])

        score(0)

        def totals(i, carry):
            top, total = carry
            s = raw[i % 2].reshape(GROUP * 4, 8, 8, TILE)
            new_top = jnp.maximum(top, jnp.max(jnp.max(s, axis=1), axis=0))
            added = jnp.sum(jnp.sum(jnp.exp2((s - new_top) * RATE), axis=1), axis=0)
            score(i + 1)
            return new_top, total * jnp.exp2((top - new_top) * RATE) + added

        top, total = lax.fori_loop(
            0, steps, totals,
            (jnp.full((8, TILE), FLOOR, jnp.float32), jnp.zeros((8, TILE), jnp.float32)),
        )
        row_top = jnp.max(top, axis=0, keepdims=True)
        row_sum = jnp.sum(total * jnp.exp2((top - row_top) * RATE), axis=0, keepdims=True)
        level_ref[t] = row_top + jnp.log2(row_sum) * (1.0 / RATE)
        return carry

    lax.fori_loop(0, tiles, tile, 0)


def prepare(core, order, count, chunk_list, first, other, key_code, query_code):
    chips = first.shape[0]
    blocks, tiles = 2 * chips, chips
    pairs = blocks * QBLK * 2048
    bf16 = jnp.bfloat16
    return pl.pallas_call(
        prepare_kernel,
        out_shape=(
            jax.ShapeDtypeStruct((blocks + 1, CHUNK, 2 * HD), bf16),
            jax.ShapeDtypeStruct((blocks, HD, CHUNK), bf16),
            jax.ShapeDtypeStruct((blocks, CHUNK, 2 * HD), bf16),
            jax.ShapeDtypeStruct((tiles, TILE, HD), bf16),
            jax.ShapeDtypeStruct((tiles, 2 * HD, TILE), bf16),
            jax.ShapeDtypeStruct((tiles, 1, TILE), jnp.float32),
        ),
        in_specs=[smem] * 4 + [vmem] * 4,
        out_specs=(vmem,) * 6,
        scratch_shapes=[pltpu.VMEM((2, GROUP, CHUNK, TILE), jnp.float32)],
        compiler_params=params,
        cost_estimate=pl.CostEstimate(
            flops=4 * pairs * HD, bytes_accessed=8 * 2**20, transcendentals=pairs
        ),
        name="prepare",
    )(core, order, count, chunk_list, first, other, key_code, query_code)


def grads_kernel(
    core_ref, order_ref, count_ref, list_ref,
    second_ref, keys, keys_t, values, qs, qt, level_ref,
    dq_ref, keep_ref, send_ref,
    gs, gt, acc_k, acc_v, acc_q,
):
    core = core_ref[0]
    chips = second_ref.shape[0]
    tiles = qs.shape[0]

    def clear(i, carry):
        acc_k[i] = jnp.zeros((CHUNK, HD), jnp.float32)
        acc_v[i] = jnp.zeros((CHUNK, HD), jnp.float32)
        return carry

    lax.fori_loop(0, 2 * chips, clear, 0)
    gt[HD + EXTRA :, :] = jnp.zeros((HD - EXTRA, TILE), jnp.bfloat16)

    def tile(t, carry):
        a, b = order_ref[2 * t], order_ref[2 * t + 1]
        count = count_ref[t]
        for slot, block in ((0, a), (1, b)):
            at = pl.multiple_of(block % 2 * QBLK, QBLK)
            g = second_ref[block // 2, pl.ds(at, QBLK), :]
            rows = slice(slot * QBLK, (slot + 1) * QBLK)
            gs[rows, :] = g
            gt[:HD, rows] = g.T
            at = pl.multiple_of(CHUNK + block % 2 * EXTRA, EXTRA)
            gt[HD : HD + EXTRA, rows] = second_ref[block // 2, pl.ds(at, EXTRA), :]
        acc_q[...] = jnp.zeros_like(acc_q)
        level = level_ref[t]

        def some(first, number):
            spots = [list_ref[t, first + u] for u in range(number)]
            scores = [dot(keys[spot], qt[t]) for spot in spots]
            slopes = [dot(values[spot], gt[...]) for spot in spots]
            low = []
            for u, spot in enumerate(spots):
                p = jnp.exp2((scores[u] - level) * RATE)
                s = (p * slopes[u]).astype(jnp.bfloat16)
                acc_v[spot] += dot(p.astype(jnp.bfloat16), gs[...])
                acc_k[spot] += dot(s, qs[t])
                low.append(s)
            left = jnp.concatenate([keys_t[spot] for spot in spots], axis=1)
            acc_q[...] += dot(left, jnp.concatenate(low, axis=0))

        def step(i, carry):
            some(GROUP * i, GROUP)
            return carry

        full = count // GROUP
        lax.fori_loop(0, full, step, 0)
        for rest in range(1, GROUP):
            pl.when(count - GROUP * full == rest)(lambda: some(GROUP * full, rest))

        result = (acc_q[...] * SCALE).T.astype(jnp.bfloat16)
        for slot, block in ((0, a), (1, b)):
            at = pl.multiple_of(block % 2 * QBLK, QBLK)
            dq_ref[block // 2, pl.ds(at, QBLK), :] = result[slot * QBLK : (slot + 1) * QBLK]
        return carry

    lax.fori_loop(0, tiles, tile, 0)

    def hand_out(i, carry):
        mine, theirs = 2 * i + core, 2 * i + 1 - core
        keep_ref[i, :CHUNK] = acc_k[mine] * SCALE
        keep_ref[i, CHUNK:] = acc_v[mine]
        send_ref[i, :CHUNK] = (acc_k[theirs] * SCALE).astype(jnp.bfloat16)
        send_ref[i, CHUNK:] = acc_v[theirs].astype(jnp.bfloat16)
        return carry

    lax.fori_loop(0, chips, hand_out, 0)


def grads(core, order, count, chunk_list, second, keys, keys_t, values, qs, qt, level):
    chips = second.shape[0]
    blocks = 2 * chips
    pairs = blocks * QBLK * 2048
    return pl.pallas_call(
        grads_kernel,
        out_shape=(
            jax.ShapeDtypeStruct((chips, TILE, HD), jnp.bfloat16),
            jax.ShapeDtypeStruct((chips, 2 * CHUNK, HD), jnp.float32),
            jax.ShapeDtypeStruct((chips, 2 * CHUNK, HD), jnp.bfloat16),
        ),
        in_specs=[smem] * 4 + [vmem] * 7,
        out_specs=(vmem,) * 3,
        scratch_shapes=[
            pltpu.VMEM((TILE, HD), jnp.bfloat16),
            pltpu.VMEM((2 * HD, TILE), jnp.bfloat16),
            pltpu.VMEM((blocks, CHUNK, HD), jnp.float32),
            pltpu.VMEM((blocks, CHUNK, HD), jnp.float32),
            pltpu.VMEM((HD, TILE), jnp.float32),
        ],
        compiler_params=params,
        cost_estimate=pl.CostEstimate(
            flops=10 * pairs * HD, bytes_accessed=10 * 2**20, transcendentals=pairs
        ),
        name="grads",
    )(core, order, count, chunk_list, second, keys, keys_t, values, qs, qt, level)


def plan(ids, lengths):
    blocks = ids.shape[0]
    ends = jnp.cumsum(lengths)
    offsets = ends - lengths
    starts, stops = (jnp.pad(x, (0, HD - x.shape[0])) for x in (offsets, ends))
    place = jnp.arange(blocks, dtype=jnp.int32)
    lanes = jnp.arange(HD, dtype=jnp.int32)
    key_tokens = jnp.arange(blocks * CHUNK, dtype=jnp.int32)[:, None]
    outside = ((key_tokens < starts) | (key_tokens >= stops)) & (lanes < lengths.shape[0])
    key_code = outside.astype(jnp.bfloat16).reshape(blocks, CHUNK, HD)

    rank = jnp.sum((ids[None, :] < ids[:, None]).astype(jnp.int32), axis=1)
    hit = (rank[None, :] == place[:, None]).astype(jnp.int32)
    order = jnp.sum(hit * place[None, :], axis=1)
    sorted_ids = jnp.sum(hit * ids[None, :], axis=1)
    tokens = (sorted_ids[:, None] * QBLK + jnp.arange(QBLK, dtype=jnp.int32)[None, :])[..., None]
    within = (tokens >= starts) & (tokens < stops)
    query_code = jnp.where(within, FLOOR, 0.0).astype(jnp.bfloat16).reshape(-1, TILE, HD)

    def bounds(token):
        inside = (token[:, None] >= offsets) & (token[:, None] < ends)
        return [jnp.sum(jnp.where(inside, x, 0), axis=1) for x in (offsets, ends)]

    first = bounds(sorted_ids * QBLK)[0] // CHUNK
    last = (bounds(sorted_ids * QBLK + QBLK - 1)[1] - 1) // CHUNK
    needed = (place[None, :] >= first[:, None]) & (place[None, :] <= last[:, None])
    needed = (needed[0::2] | needed[1::2]).astype(jnp.int32)
    count = jnp.sum(needed, axis=1)
    before = jnp.sum(needed[:, None, :] * (place[None, :] < place[:, None]), axis=2)
    slots = jnp.arange(blocks + GROUP, dtype=jnp.int32)
    chosen = (before[:, None, :] == slots[None, :, None]) & (needed[:, None, :] > 0)
    chunk_list = jnp.sum(jnp.where(chosen, place[None, None, :], 0), axis=2)
    chunk_list = jnp.where(slots[None, :] < count[:, None], chunk_list, blocks)
    return order, count, chunk_list, key_code, query_code


def split_in_three(x):
    parts = []
    for _ in range(3):
        part = lax.reduce_precision(x, exponent_bits=8, mantissa_bits=7)
        parts.append(part.astype(jnp.bfloat16))
        x = x - part
    return jnp.stack(parts, axis=-2)


def on_device(queries, keys_in, values_in, forward_out, grad_out, lengths, query_block):
    size = lax.axis_size("seq")
    chips = size // 2
    core = lax.axis_index("seq") % 2
    rows = queries.shape[0]
    heads = queries.shape[1] // HD
    groups = [[2 * i + c for i in range(chips)] for c in range(2)]
    swap = [(i, i ^ 1) for i in range(size)]

    def exchange(x):
        return lax.all_to_all(x, "seq", 0, 0, axis_index_groups=groups)

    ids = jnp.broadcast_to(query_block.astype(jnp.bfloat16)[:, None], (2, HD))
    ids = jnp.pad(ids, ((0, EXTRA - 2), (0, 0)))
    first = exchange(pack(ids, keys_in, values_in, queries, chips))

    delta = jnp.sum(
        (grad_out.astype(jnp.float32) * forward_out.astype(jnp.float32)).reshape(rows, heads, HD),
        axis=2,
    )
    parts = split_in_three(delta.T.reshape(heads, rows // QBLK, QBLK))
    parts = jnp.pad(parts, ((0, 0), (0, 0), (0, EXTRA - 3), (0, 0))).reshape(heads, -1, HD)
    second = jnp.concatenate(
        [grad_out.reshape(rows, heads, HD).transpose(1, 0, 2), parts], axis=1
    )
    second = jnp.pad(second, ((0, chips - heads), (0, 0), (0, 0)))
    first, second = lax.optimization_barrier((first, second))
    second = exchange(second)

    ids = first[:, 3 * rows : 3 * rows + 2, 0].astype(jnp.int32).reshape(-1)
    order, count, chunk_list, key_code, query_code = plan(ids, lengths)
    other = lax.ppermute(first[:, : 2 * rows], "seq", swap)
    core_arg = jnp.full((1,), core, jnp.int32)
    ready = prepare(core_arg, order, count, chunk_list, first, other, key_code, query_code)
    dq, keep, send = grads(core_arg, order, count, chunk_list, second, *ready)

    received = lax.ppermute(send, "seq", swap)
    dq = exchange(dq)
    dkv = exchange((keep + received.astype(jnp.float32)).astype(jnp.bfloat16))

    def by_row(x):
        return x[:heads].transpose(1, 0, 2).reshape(rows, heads * HD)

    return by_row(dq), by_row(dkv[:, :rows]), by_row(dkv[:, rows:])


def solution(mesh):
    spec = P(("win", "seq"), "head")
    in_specs = (spec,) * 5 + (P("win"), P(("win", "seq")))
    return jax.shard_map(
        on_device, mesh=mesh, in_specs=in_specs, out_specs=(spec,) * 3, check_vma=False
    )
```

```python
import math

import jax
import jax.numpy as jnp
from jax import lax
from jax.experimental import pallas as pl
from jax.experimental.pallas import tpu as pltpu
from jax.sharding import PartitionSpec as P

HD = 128
QBLK = 128
CHUNK = 256
TILE = 2 * QBLK
GROUP = 3
SCALE = HD ** (-0.5)
RATE = SCALE * math.log2(math.e)
FLOOR = -1e30
EXTRA = 16

smem = pl.BlockSpec(memory_space=pltpu.SMEM)
vmem = pl.BlockSpec(memory_space=pltpu.VMEM)
params = pltpu.CompilerParams(vmem_limit_bytes=16 * 1024 * 1024)


def dot(a, b):
    return jnp.dot(a, b, preferred_element_type=jnp.float32)


def pack_kernel(ids_ref, k_ref, q_ref, out_ref):
    rows = k_ref.shape[0]
    heads = k_ref.shape[1] // HD
    line = lax.broadcasted_iota(jnp.int32, (EXTRA, HD), 0)
    note = jnp.where(line == 0, ids_ref[0], ids_ref[1]).astype(jnp.float32).astype(out_ref.dtype)
    for slot in range(out_ref.shape[0]):
        columns = slice(slot % heads * HD, (slot % heads + 1) * HD)
        out_ref[slot, :rows, :] = k_ref[:, columns]
        out_ref[slot, rows : 2 * rows, :] = q_ref[:, columns]
        out_ref[slot, 2 * rows :, :] = note


def pack(ids, k, q, chips):
    rows = k.shape[0]
    return pl.pallas_call(
        pack_kernel,
        out_shape=jax.ShapeDtypeStruct((chips, 2 * rows + EXTRA, HD), k.dtype),
        in_specs=[smem, vmem, vmem],
        out_specs=vmem,
        name="pack",
    )(ids, k, q)


def unpack_kernel(x_ref, *out_refs):
    rows, width = out_refs[0].shape
    for i, out_ref in enumerate(out_refs):
        for head in range(width // HD):
            columns = slice(head * HD, (head + 1) * HD)
            out_ref[:, columns] = x_ref[head, i * rows : (i + 1) * rows, :]


def unpack(x, rows, heads):
    number = x.shape[1] // rows
    return pl.pallas_call(
        unpack_kernel,
        out_shape=(jax.ShapeDtypeStruct((rows, heads * HD), x.dtype),) * number,
        in_specs=[vmem],
        out_specs=(vmem,) * number,
        name="unpack",
    )(x)


def place_key(keys, spot, k, edges):
    rows = lax.broadcasted_iota(jnp.int32, (CHUNK, HD), 0) + spot * CHUNK
    outside = (rows < edges[0:1]) | (rows >= edges[1:2])
    keys[spot, :, :HD] = k
    keys[spot, :, HD:] = jnp.where(outside, 1.0, 0.0).astype(jnp.bfloat16)


def place_query(qt, slot, q, token, sides):
    rows = slice(slot * QBLK, (slot + 1) * QBLK)
    tokens = lax.broadcasted_iota(jnp.int32, (EXTRA, QBLK), 1) + token
    within = (tokens >= sides[:EXTRA]) & (tokens < sides[EXTRA:])
    qt[:HD, rows] = q.T
    qt[HD : HD + EXTRA, rows] = jnp.where(within, FLOOR, 0.0).astype(jnp.bfloat16)


def block_rows(block, base, size):
    return pl.ds(pl.multiple_of(base + block % 2 * size, size), size)


def prepare_kernel(
    core_ref, order_ref, token_ref, count_ref, list_ref, first_ref, other_ref, edges, sides,
    level_ref,
    keys, qt, raw,
):
    core = core_ref[0]
    chips = first_ref.shape[0]
    tiles = level_ref.shape[0]

    def place(i, carry):
        place_key(keys, 2 * i + core, first_ref[i, :CHUNK, :], edges)
        place_key(keys, 2 * i + 1 - core, other_ref[i], edges)
        return carry

    lax.fori_loop(0, chips, place, 0)
    keys[2 * chips] = jnp.ones((CHUNK, 2 * HD), jnp.bfloat16)
    qt[HD:, :] = jnp.zeros((HD, TILE), jnp.bfloat16)

    def tile(t, carry):
        for slot in range(2):
            block = order_ref[2 * t + slot]
            q = first_ref[block // 2, block_rows(block, CHUNK, QBLK), :]
            place_query(qt, slot, q, token_ref[2 * t + slot], sides)
        steps = (count_ref[t] + GROUP - 1) // GROUP

        def score(i):
            i = jnp.minimum(i, steps - 1)
            for u in range(GROUP):
                raw[i % 2, u] = dot(keys[list_ref[t, GROUP * i + u]], qt[...])

        score(0)

        def totals(i, carry):
            top, total = carry
            s = raw[i % 2].reshape(GROUP * 4, 8, 8, TILE)
            new_top = jnp.maximum(top, jnp.max(jnp.max(s, axis=1), axis=0))
            added = jnp.sum(jnp.sum(jnp.exp2((s - new_top) * RATE), axis=1), axis=0)
            score(i + 1)
            return new_top, total * jnp.exp2((top - new_top) * RATE) + added

        top, total = lax.fori_loop(
            0, steps, totals,
            (jnp.full((8, TILE), FLOOR, jnp.float32), jnp.zeros((8, TILE), jnp.float32)),
        )
        row_top = jnp.max(top, axis=0, keepdims=True)
        row_sum = jnp.sum(total * jnp.exp2((top - row_top) * RATE), axis=0, keepdims=True)
        level_ref[t] = row_top + jnp.log2(row_sum) * (1.0 / RATE)
        return carry

    lax.fori_loop(0, tiles, tile, 0)


def prepare(scalars, first, other, edges, sides):
    chips = first.shape[0]
    blocks, tiles = 2 * chips, chips
    pairs = blocks * QBLK * 2048
    return pl.pallas_call(
        prepare_kernel,
        out_shape=jax.ShapeDtypeStruct((tiles, 1, TILE), jnp.float32),
        in_specs=[smem] * len(scalars) + [vmem] * 4,
        out_specs=vmem,
        scratch_shapes=[
            pltpu.VMEM((blocks + 1, CHUNK, 2 * HD), jnp.bfloat16),
            pltpu.VMEM((2 * HD, TILE), jnp.bfloat16),
            pltpu.VMEM((2, GROUP, CHUNK, TILE), jnp.float32),
        ],
        compiler_params=params,
        cost_estimate=pl.CostEstimate(
            flops=4 * pairs * HD, bytes_accessed=8 * 2**20, transcendentals=pairs
        ),
        name="prepare",
    )(*scalars, first, other, edges, sides)


def grads_kernel(
    core_ref, order_ref, token_ref, count_ref, list_ref, first_ref, other_ref, edges, sides,
    second_ref, second_other, level_ref,
    dq_ref, keep_ref, send_ref,
    keys, keys_t, values, qs, qt, gs, gt, acc_k, acc_v, acc_q,
):
    core = core_ref[0]
    chips = first_ref.shape[0]
    tiles = level_ref.shape[0]

    def place(i, carry):
        mine, theirs = 2 * i + core, 2 * i + 1 - core
        for spot, k, v in (
            (mine, first_ref[i, :CHUNK, :], second_ref[i, :CHUNK, :]),
            (theirs, other_ref[i], second_other[i]),
        ):
            place_key(keys, spot, k, edges)
            keys_t[spot] = k.T
            values[spot, :, :HD] = v
            values[spot, :, HD:] = jnp.full((CHUNK, HD), -1, jnp.bfloat16)
            acc_k[spot] = jnp.zeros((CHUNK, HD), jnp.float32)
            acc_v[spot] = jnp.zeros((CHUNK, HD), jnp.float32)
        return carry

    lax.fori_loop(0, chips, place, 0)
    qt[HD:, :] = jnp.zeros((HD, TILE), jnp.bfloat16)
    gt[HD:, :] = jnp.zeros((HD, TILE), jnp.bfloat16)

    def tile(t, carry):
        count = count_ref[t]
        blocks = [order_ref[2 * t + slot] for slot in range(2)]
        for slot, block in enumerate(blocks):
            rows = slice(slot * QBLK, (slot + 1) * QBLK)
            q = first_ref[block // 2, block_rows(block, CHUNK, QBLK), :]
            g = second_ref[block // 2, block_rows(block, CHUNK, QBLK), :]
            qs[rows, :] = q
            gs[rows, :] = g
            place_query(qt, slot, q, token_ref[2 * t + slot], sides)
            gt[:HD, rows] = g.T
            gt[HD : HD + EXTRA, rows] = second_ref[block // 2, block_rows(block, 2 * CHUNK, EXTRA), :]
        acc_q[...] = jnp.zeros_like(acc_q)
        level = level_ref[t]

        def some(first, number):
            spots = [list_ref[t, first + u] for u in range(number)]
            scores = [dot(keys[spot], qt[...]) for spot in spots]
            slopes = [dot(values[spot], gt[...]) for spot in spots]
            low = []
            for u, spot in enumerate(spots):
                p = jnp.exp2((scores[u] - level) * RATE)
                s = (p * slopes[u]).astype(jnp.bfloat16)
                acc_v[spot] += dot(p.astype(jnp.bfloat16), gs[...])
                acc_k[spot] += dot(s, qs[...])
                low.append(s)
            left = jnp.concatenate([keys_t[spot] for spot in spots], axis=1)
            acc_q[...] += dot(left, jnp.concatenate(low, axis=0))

        def step(i, carry):
            some(GROUP * i, GROUP)
            return carry

        full = count // GROUP
        lax.fori_loop(0, full, step, 0)
        for rest in range(1, GROUP):
            pl.when(count - GROUP * full == rest)(lambda: some(GROUP * full, rest))

        result = (acc_q[...] * SCALE).T.astype(jnp.bfloat16)
        for slot, block in enumerate(blocks):
            part = result[slot * QBLK : (slot + 1) * QBLK]
            dq_ref[block // 2, block_rows(block, 0, QBLK), :] = part
        return carry

    lax.fori_loop(0, tiles, tile, 0)

    def hand_out(i, carry):
        mine, theirs = 2 * i + core, 2 * i + 1 - core
        keep_ref[i, :CHUNK] = acc_k[mine] * SCALE
        keep_ref[i, CHUNK:] = acc_v[mine]
        send_ref[i, :CHUNK] = (acc_k[theirs] * SCALE).astype(jnp.bfloat16)
        send_ref[i, CHUNK:] = acc_v[theirs].astype(jnp.bfloat16)
        return carry

    lax.fori_loop(0, chips, hand_out, 0)


def grads(scalars, first, other, edges, sides, second, second_other, level):
    chips = second.shape[0]
    blocks = 2 * chips
    pairs = blocks * QBLK * 2048
    bf16 = jnp.bfloat16
    return pl.pallas_call(
        grads_kernel,
        out_shape=(
            jax.ShapeDtypeStruct((chips, TILE, HD), bf16),
            jax.ShapeDtypeStruct((chips, 2 * CHUNK, HD), jnp.float32),
            jax.ShapeDtypeStruct((chips, 2 * CHUNK, HD), bf16),
        ),
        in_specs=[smem] * len(scalars) + [vmem] * 7,
        out_specs=(vmem,) * 3,
        scratch_shapes=[
            pltpu.VMEM((blocks, CHUNK, 2 * HD), bf16),
            pltpu.VMEM((blocks, HD, CHUNK), bf16),
            pltpu.VMEM((blocks, CHUNK, 2 * HD), bf16),
            pltpu.VMEM((TILE, HD), bf16),
            pltpu.VMEM((2 * HD, TILE), bf16),
            pltpu.VMEM((TILE, HD), bf16),
            pltpu.VMEM((2 * HD, TILE), bf16),
            pltpu.VMEM((blocks, CHUNK, HD), jnp.float32),
            pltpu.VMEM((blocks, CHUNK, HD), jnp.float32),
            pltpu.VMEM((HD, TILE), jnp.float32),
        ],
        compiler_params=params,
        cost_estimate=pl.CostEstimate(
            flops=10 * pairs * HD, bytes_accessed=10 * 2**20, transcendentals=pairs
        ),
        name="grads",
    )(*scalars, first, other, edges, sides, second, second_other, level)


def plan(ids, lengths):
    blocks = ids.shape[0]
    ends = jnp.cumsum(lengths)
    offsets = ends - lengths
    place = jnp.arange(blocks, dtype=jnp.int32)
    rank = jnp.sum((ids[None, :] < ids[:, None]).astype(jnp.int32), axis=1)
    hit = (rank[None, :] == place[:, None]).astype(jnp.int32)
    order = jnp.sum(hit * place[None, :], axis=1)
    tokens = jnp.sum(hit * ids[None, :], axis=1) * QBLK

    def bounds(token):
        inside = (token[:, None] >= offsets) & (token[:, None] < ends)
        return [jnp.sum(jnp.where(inside, x, 0), axis=1) for x in (offsets, ends)]

    first = bounds(tokens)[0] // CHUNK
    last = (bounds(tokens + QBLK - 1)[1] - 1) // CHUNK
    needed = (place[None, :] >= first[:, None]) & (place[None, :] <= last[:, None])
    needed = (needed[0::2] | needed[1::2]).astype(jnp.int32)
    count = jnp.sum(needed, axis=1)
    before = jnp.sum(needed[:, None, :] * (place[None, :] < place[:, None]), axis=2)
    slots = jnp.arange(blocks + GROUP, dtype=jnp.int32)
    chosen = (before[:, None, :] == slots[None, :, None]) & (needed[:, None, :] > 0)
    chunk_list = jnp.sum(jnp.where(chosen, place[None, None, :], 0), axis=2)
    chunk_list = jnp.where(slots[None, :] < count[:, None], chunk_list, blocks)
    return order, tokens, count, chunk_list


def edges_of(lengths, tokens):
    ends = jnp.cumsum(lengths)
    offsets = ends - lengths
    spare = HD - lengths.shape[0]
    edges = jnp.stack([jnp.pad(offsets, (0, spare)), jnp.pad(ends, (0, spare), constant_values=tokens)])
    spare = EXTRA - lengths.shape[0]
    sides = [jnp.pad(x, (0, spare), constant_values=tokens) for x in (offsets, ends)]
    return edges, jnp.broadcast_to(jnp.concatenate(sides)[:, None], (2 * EXTRA, QBLK))


def split_in_three(x):
    parts = []
    for _ in range(3):
        part = lax.reduce_precision(x, exponent_bits=8, mantissa_bits=7)
        parts.append(part.astype(jnp.bfloat16))
        x = x - part
    return jnp.stack(parts, axis=-2)


def on_device(queries, keys_in, values_in, forward_out, grad_out, lengths, query_block):
    size = lax.axis_size("seq")
    chips = size // 2
    core = lax.axis_index("seq") % 2
    rows = queries.shape[0]
    heads = queries.shape[1] // HD
    groups = [[2 * i + c for i in range(chips)] for c in range(2)]
    swap = [(i, i ^ 1) for i in range(size)]

    def exchange(x):
        return lax.all_to_all(x, "seq", 0, 0, axis_index_groups=groups)

    first = exchange(pack(query_block, keys_in, queries, chips))

    delta = jnp.sum(
        (grad_out.astype(jnp.float32) * forward_out.astype(jnp.float32)).reshape(rows, heads, HD),
        axis=2,
    )
    parts = split_in_three(delta.T.reshape(heads, rows // QBLK, QBLK))
    parts = jnp.pad(parts, ((0, 0), (0, 0), (0, EXTRA - 3), (0, 0))).reshape(heads, -1, HD)
    by_head = [x.reshape(rows, heads, HD).transpose(1, 0, 2) for x in (values_in, grad_out)]
    second = jnp.concatenate(by_head + [parts], axis=1)
    second = jnp.pad(second, ((0, chips - heads), (0, 0), (0, 0)))
    first, second = lax.optimization_barrier((first, second))
    second = exchange(second)

    ids = first[:, 2 * rows : 2 * rows + 2, 0].astype(jnp.int32).reshape(-1)
    scalars = (jnp.full((1,), core, jnp.int32), *plan(ids, lengths))
    edges, sides = edges_of(lengths, size * rows)
    other = lax.ppermute(first[:, :rows], "seq", swap)
    level = prepare(scalars, first, other, edges, sides)
    second, level = lax.optimization_barrier((second, level))
    second_other = lax.ppermute(second[:, :rows], "seq", swap)
    dq, keep, send = grads(
        scalars, first, other, edges, sides, second, second_other, level
    )

    received = lax.ppermute(send, "seq", swap)
    dkv = (keep + received.astype(jnp.float32)).astype(jnp.bfloat16)
    return unpack(exchange(jnp.concatenate([dq, dkv], axis=1)), rows, heads)


def solution(mesh):
    spec = P(("win", "seq"), "head")
    in_specs = (spec,) * 5 + (P("win"), P(("win", "seq")))
    return jax.shard_map(
        on_device, mesh=mesh, in_specs=in_specs, out_specs=(spec,) * 3, check_vma=False
    )
```

```python
import math

import jax
import jax.numpy as jnp
from jax import lax
from jax.experimental import pallas as pl
from jax.experimental.pallas import tpu as pltpu
from jax.sharding import PartitionSpec as P

HD = 128
QBLK = 128
CHUNK = 256
TILE = 2 * QBLK
GROUP = 4
SCALE = HD ** (-0.5)
RATE = SCALE * math.log2(math.e)
FLOOR = -1e30
EXTRA = 16

smem = pl.BlockSpec(memory_space=pltpu.SMEM)
vmem = pl.BlockSpec(memory_space=pltpu.VMEM)
params = pltpu.CompilerParams(vmem_limit_bytes=32 * 1024 * 1024)


def dot(a, b):
    return jnp.dot(a, b, preferred_element_type=jnp.float32)


def pack_kernel(ids_ref, k_ref, q_ref, out_ref):
    rows = k_ref.shape[0]
    heads = k_ref.shape[1] // HD
    line = lax.broadcasted_iota(jnp.int32, (EXTRA, HD), 0)
    note = jnp.where(line == 0, ids_ref[0], ids_ref[1]).astype(jnp.float32).astype(out_ref.dtype)
    for slot in range(out_ref.shape[0]):
        columns = slice(slot % heads * HD, (slot % heads + 1) * HD)
        out_ref[slot, :rows, :] = k_ref[:, columns]
        out_ref[slot, rows : 2 * rows, :] = q_ref[:, columns]
        out_ref[slot, 2 * rows :, :] = note


def pack(ids, k, q, chips):
    rows = k.shape[0]
    return pl.pallas_call(
        pack_kernel,
        out_shape=jax.ShapeDtypeStruct((chips, 2 * rows + EXTRA, HD), k.dtype),
        in_specs=[smem, vmem, vmem],
        out_specs=vmem,
        name="pack",
    )(ids, k, q)


def unpack_kernel(x_ref, *out_refs):
    rows, width = out_refs[0].shape
    for i, out_ref in enumerate(out_refs):
        for head in range(width // HD):
            columns = slice(head * HD, (head + 1) * HD)
            out_ref[:, columns] = x_ref[head, i * rows : (i + 1) * rows, :]


def unpack(x, rows, heads):
    number = x.shape[1] // rows
    return pl.pallas_call(
        unpack_kernel,
        out_shape=(jax.ShapeDtypeStruct((rows, heads * HD), x.dtype),) * number,
        in_specs=[vmem],
        out_specs=(vmem,) * number,
        name="unpack",
    )(x)


def place_key(keys, spot, k, edges):
    rows = lax.broadcasted_iota(jnp.int32, (CHUNK, HD), 0) + spot * CHUNK
    outside = (rows < edges[0:1]) | (rows >= edges[1:2])
    keys[spot, :, :HD] = k
    keys[spot, :, HD:] = jnp.where(outside, 1.0, 0.0).astype(jnp.bfloat16)


def place_query(qt, slot, q, token, sides):
    rows = slice(slot * QBLK, (slot + 1) * QBLK)
    tokens = lax.broadcasted_iota(jnp.int32, (EXTRA, QBLK), 1) + token
    within = (tokens >= sides[:EXTRA]) & (tokens < sides[EXTRA:])
    qt[:HD, rows] = q.T
    qt[HD : HD + EXTRA, rows] = jnp.where(within, FLOOR, 0.0).astype(jnp.bfloat16)


def block_rows(block, base, size):
    return pl.ds(pl.multiple_of(base + block % 2 * size, size), size)


def prepare_kernel(
    core_ref, order_ref, token_ref, steps_ref, tile_ref, spot_ref, first_ref, other_ref, edges, sides,
    level_ref,
    keys, qt, raw, tops, totals,
):
    core = core_ref[0]
    chips = first_ref.shape[0]
    tiles = level_ref.shape[0]

    def place(i, carry):
        place_key(keys, 2 * i + core, first_ref[i, :CHUNK, :], edges)
        place_key(keys, 2 * i + 1 - core, other_ref[i], edges)
        for slot in range(2):
            block = order_ref[2 * i + slot]
            q = first_ref[block // 2, block_rows(block, CHUNK, QBLK), :]
            place_query(qt.at[i], slot, q, token_ref[2 * i + slot], sides)
        qt[i, HD + EXTRA :, :] = jnp.zeros((HD - EXTRA, TILE), jnp.bfloat16)
        tops[i] = jnp.full((8, TILE), FLOOR, jnp.float32)
        totals[i] = jnp.zeros((8, TILE), jnp.float32)
        return carry

    lax.fori_loop(0, chips, place, 0)
    keys[2 * chips] = jnp.ones((CHUNK, 2 * HD), jnp.bfloat16)

    def score(i, u):
        return dot(keys[spot_ref[GROUP * i + u]], qt[tile_ref[GROUP * i + u]])

    for u in range(GROUP):
        raw[0, u] = score(0, u)

    def step(i, carry):
        parts = []
        for u in range(GROUP):
            s = raw[i % 2, u].reshape(4, 8, 8, TILE)
            top = jnp.max(jnp.max(s, axis=1), axis=0)
            total = jnp.sum(jnp.sum(jnp.exp2((s - top) * RATE), axis=1), axis=0)
            parts.append((top, total))
        for u in range(GROUP):
            raw[(i + 1) % 2, u] = score(i + 1, u)
        for u, (top, total) in enumerate(parts):
            t = tile_ref[GROUP * i + u]
            old = tops[t]
            new = jnp.maximum(old, top)
            totals[t] = totals[t] * jnp.exp2((old - new) * RATE) + total * jnp.exp2((top - new) * RATE)
            tops[t] = new
        return carry

    lax.fori_loop(0, steps_ref[0], step, 0)
    for t in range(tiles):
        top = tops[t]
        row_top = jnp.max(top, axis=0, keepdims=True)
        row_sum = jnp.sum(totals[t] * jnp.exp2((top - row_top) * RATE), axis=0, keepdims=True)
        level_ref[t] = row_top + jnp.log2(row_sum) * (1.0 / RATE)


def prepare(scalars, first, other, edges, sides):
    chips = first.shape[0]
    blocks, tiles = 2 * chips, chips
    pairs = blocks * QBLK * 2048
    return pl.pallas_call(
        prepare_kernel,
        out_shape=jax.ShapeDtypeStruct((tiles, 1, TILE), jnp.float32),
        in_specs=[smem] * len(scalars) + [vmem] * 4,
        out_specs=vmem,
        scratch_shapes=[
            pltpu.VMEM((blocks + 1, CHUNK, 2 * HD), jnp.bfloat16),
            pltpu.VMEM((tiles, 2 * HD, TILE), jnp.bfloat16),
            pltpu.VMEM((2, GROUP, CHUNK, TILE), jnp.float32),
            pltpu.VMEM((tiles, 8, TILE), jnp.float32),
            pltpu.VMEM((tiles, 8, TILE), jnp.float32),
        ],
        compiler_params=params,
        cost_estimate=pl.CostEstimate(
            flops=4 * pairs * HD, bytes_accessed=8 * 2**20, transcendentals=pairs
        ),
        name="prepare",
    )(*scalars, first, other, edges, sides)


def grads_kernel(
    core_ref, order_ref, token_ref, steps_ref, tile_ref, spot_ref, first_ref, other_ref, edges, sides,
    second_ref, second_other, level_ref,
    dq_ref, keep_ref, send_ref,
    keys, keys_t, values, qs, qt, gs, gt, raw, slope, acc_k, acc_v, acc_q,
):
    core = core_ref[0]
    chips = first_ref.shape[0]
    tiles = level_ref.shape[0]

    def place(i, carry):
        mine, theirs = 2 * i + core, 2 * i + 1 - core
        for spot, k, v in (
            (mine, first_ref[i, :CHUNK, :], second_ref[i, :CHUNK, :]),
            (theirs, other_ref[i], second_other[i]),
        ):
            place_key(keys, spot, k, edges)
            keys_t[spot] = k.T
            values[spot, :, :HD] = v
            values[spot, :, HD:] = jnp.full((CHUNK, HD), -1, jnp.bfloat16)
            acc_k[spot] = jnp.zeros((CHUNK, HD), jnp.float32)
            acc_v[spot] = jnp.zeros((CHUNK, HD), jnp.float32)
        acc_q[i] = jnp.zeros((HD, TILE), jnp.float32)
        for slot in range(2):
            block = order_ref[2 * i + slot]
            rows = slice(slot * QBLK, (slot + 1) * QBLK)
            q = first_ref[block // 2, block_rows(block, CHUNK, QBLK), :]
            g = second_ref[block // 2, block_rows(block, CHUNK, QBLK), :]
            qs[i, rows, :] = q
            gs[i, rows, :] = g
            place_query(qt.at[i], slot, q, token_ref[2 * i + slot], sides)
            gt[i, :HD, rows] = g.T
            delta = second_ref[block // 2, block_rows(block, 2 * CHUNK, EXTRA), :]
            gt[i, HD : HD + EXTRA, rows] = delta
        for ref in (qt, gt):
            ref[i, HD + EXTRA :, :] = jnp.zeros((HD - EXTRA, TILE), jnp.bfloat16)
        return carry

    lax.fori_loop(0, chips, place, 0)
    none = 2 * chips
    keys[none] = jnp.ones((CHUNK, 2 * HD), jnp.bfloat16)
    keys_t[none] = jnp.zeros((HD, CHUNK), jnp.bfloat16)
    values[none] = jnp.zeros((CHUNK, 2 * HD), jnp.bfloat16)
    acc_k[none] = jnp.zeros((CHUNK, HD), jnp.float32)
    acc_v[none] = jnp.zeros((CHUNK, HD), jnp.float32)

    def unit(i, u):
        return tile_ref[GROUP * i + u], spot_ref[GROUP * i + u]

    def ahead(i):
        for u in range(GROUP):
            t, spot = unit(i, u)
            raw[i % 2, u] = dot(keys[spot], qt[t])
            slope[i % 2, u] = dot(values[spot], gt[t])

    ahead(0)

    def step(i, carry):
        for u in range(GROUP):
            t, spot = unit(i, u)
            p = jnp.exp2((raw[i % 2, u] - level_ref[t]) * RATE)
            s = (p * slope[i % 2, u]).astype(jnp.bfloat16)
            acc_v[spot] += dot(p.astype(jnp.bfloat16), gs[t])
            acc_k[spot] += dot(s, qs[t])
            acc_q[t] += dot(keys_t[spot], s)
        ahead(i + 1)
        return carry

    lax.fori_loop(0, steps_ref[0], step, 0)

    def hand_out(i, carry):
        mine, theirs = 2 * i + core, 2 * i + 1 - core
        keep_ref[i, :CHUNK] = acc_k[mine] * SCALE
        keep_ref[i, CHUNK:] = acc_v[mine]
        send_ref[i, :CHUNK] = (acc_k[theirs] * SCALE).astype(jnp.bfloat16)
        send_ref[i, CHUNK:] = acc_v[theirs].astype(jnp.bfloat16)
        result = (acc_q[i] * SCALE).T.astype(jnp.bfloat16)
        for slot in range(2):
            block = order_ref[2 * i + slot]
            part = result[slot * QBLK : (slot + 1) * QBLK]
            dq_ref[block // 2, block_rows(block, 0, QBLK), :] = part
        return carry

    lax.fori_loop(0, chips, hand_out, 0)


def grads(scalars, first, other, edges, sides, second, second_other, level):
    chips = second.shape[0]
    blocks, tiles = 2 * chips, chips
    pairs = blocks * QBLK * 2048
    bf16, f32 = jnp.bfloat16, jnp.float32
    return pl.pallas_call(
        grads_kernel,
        out_shape=(
            jax.ShapeDtypeStruct((chips, TILE, HD), bf16),
            jax.ShapeDtypeStruct((chips, 2 * CHUNK, HD), f32),
            jax.ShapeDtypeStruct((chips, 2 * CHUNK, HD), bf16),
        ),
        in_specs=[smem] * len(scalars) + [vmem] * 7,
        out_specs=(vmem,) * 3,
        scratch_shapes=[
            pltpu.VMEM((blocks + 1, CHUNK, 2 * HD), bf16),
            pltpu.VMEM((blocks + 1, HD, CHUNK), bf16),
            pltpu.VMEM((blocks + 1, CHUNK, 2 * HD), bf16),
            pltpu.VMEM((tiles, TILE, HD), bf16),
            pltpu.VMEM((tiles, 2 * HD, TILE), bf16),
            pltpu.VMEM((tiles, TILE, HD), bf16),
            pltpu.VMEM((tiles, 2 * HD, TILE), bf16),
            pltpu.VMEM((2, GROUP, CHUNK, TILE), f32),
            pltpu.VMEM((2, GROUP, CHUNK, TILE), f32),
            pltpu.VMEM((blocks + 1, CHUNK, HD), f32),
            pltpu.VMEM((blocks + 1, CHUNK, HD), f32),
            pltpu.VMEM((tiles, HD, TILE), f32),
        ],
        compiler_params=params,
        cost_estimate=pl.CostEstimate(
            flops=10 * pairs * HD, bytes_accessed=10 * 2**20, transcendentals=pairs
        ),
        name="grads",
    )(*scalars, first, other, edges, sides, second, second_other, level)


def plan(ids, lengths):
    blocks = ids.shape[0]
    ends = jnp.cumsum(lengths)
    offsets = ends - lengths
    place = jnp.arange(blocks, dtype=jnp.int32)
    rank = jnp.sum((ids[None, :] < ids[:, None]).astype(jnp.int32), axis=1)
    hit = (rank[None, :] == place[:, None]).astype(jnp.int32)
    order = jnp.sum(hit * place[None, :], axis=1)
    tokens = jnp.sum(hit * ids[None, :], axis=1) * QBLK

    def bounds(token):
        inside = (token[:, None] >= offsets) & (token[:, None] < ends)
        return [jnp.sum(jnp.where(inside, x, 0), axis=1) for x in (offsets, ends)]

    first = bounds(tokens)[0] // CHUNK
    last = (bounds(tokens + QBLK - 1)[1] - 1) // CHUNK
    needed = (place[None, :] >= first[:, None]) & (place[None, :] <= last[:, None])
    needed = (needed[0::2] | needed[1::2]).astype(jnp.int32).reshape(-1)
    cells = jnp.arange(needed.shape[0], dtype=jnp.int32)
    before = jnp.sum(needed[None, :] * (cells[None, :] < cells[:, None]), axis=1)
    slots = jnp.arange(needed.shape[0] + 2 * GROUP, dtype=jnp.int32)
    chosen = (before[None, :] == slots[:, None]) & (needed[None, :] > 0)
    cell = jnp.sum(jnp.where(chosen, cells[None, :], 0), axis=1)
    total = jnp.sum(needed, keepdims=True)
    tile = cell // blocks
    spot = jnp.where(slots < total, cell % blocks, blocks)
    return order, tokens, (total + GROUP - 1) // GROUP, tile, spot


def edges_of(lengths, tokens):
    ends = jnp.cumsum(lengths)
    offsets = ends - lengths
    spare = HD - lengths.shape[0]
    edges = jnp.stack([jnp.pad(offsets, (0, spare)), jnp.pad(ends, (0, spare), constant_values=tokens)])
    spare = EXTRA - lengths.shape[0]
    sides = [jnp.pad(x, (0, spare), constant_values=tokens) for x in (offsets, ends)]
    return edges, jnp.broadcast_to(jnp.concatenate(sides)[:, None], (2 * EXTRA, QBLK))


def split_in_three(x):
    parts = []
    for _ in range(3):
        part = lax.reduce_precision(x, exponent_bits=8, mantissa_bits=7)
        parts.append(part.astype(jnp.bfloat16))
        x = x - part
    return jnp.stack(parts, axis=-2)


def on_device(queries, keys_in, values_in, forward_out, grad_out, lengths, query_block):
    size = lax.axis_size("seq")
    chips = size // 2
    core = lax.axis_index("seq") % 2
    rows = queries.shape[0]
    heads = queries.shape[1] // HD
    groups = [[2 * i + c for i in range(chips)] for c in range(2)]
    swap = [(i, i ^ 1) for i in range(size)]

    def exchange(x):
        return lax.all_to_all(x, "seq", 0, 0, axis_index_groups=groups)

    first = exchange(pack(query_block, keys_in, queries, chips))

    delta = jnp.sum(
        (grad_out.astype(jnp.float32) * forward_out.astype(jnp.float32)).reshape(rows, heads, HD),
        axis=2,
    )
    parts = split_in_three(delta.T.reshape(heads, rows // QBLK, QBLK))
    parts = jnp.pad(parts, ((0, 0), (0, 0), (0, EXTRA - 3), (0, 0))).reshape(heads, -1, HD)
    by_head = [x.reshape(rows, heads, HD).transpose(1, 0, 2) for x in (values_in, grad_out)]
    second = jnp.concatenate(by_head + [parts], axis=1)
    second = jnp.pad(second, ((0, chips - heads), (0, 0), (0, 0)))
    first, second = lax.optimization_barrier((first, second))
    second = exchange(second)

    ids = first[:, 2 * rows : 2 * rows + 2, 0].astype(jnp.int32).reshape(-1)
    scalars = (jnp.full((1,), core, jnp.int32), *plan(ids, lengths))
    edges, sides = edges_of(lengths, size * rows)
    other = lax.ppermute(first[:, :rows], "seq", swap)
    level = prepare(scalars, first, other, edges, sides)
    second, level = lax.optimization_barrier((second, level))
    second_other = lax.ppermute(second[:, :rows], "seq", swap)
    dq, keep, send = grads(
        scalars, first, other, edges, sides, second, second_other, level
    )

    received = lax.ppermute(send, "seq", swap)
    dkv = (keep + received.astype(jnp.float32)).astype(jnp.bfloat16)
    return unpack(exchange(jnp.concatenate([dq, dkv], axis=1)), rows, heads)


def solution(mesh):
    spec = P(("win", "seq"), "head")
    in_specs = (spec,) * 5 + (P("win"), P(("win", "seq")))
    return jax.shard_map(
        on_device, mesh=mesh, in_specs=in_specs, out_specs=(spec,) * 3, check_vma=False
    )
```

```python
import math

import jax
import jax.numpy as jnp
from jax import lax
from jax.experimental import pallas as pl
from jax.experimental.pallas import tpu as pltpu
from jax.sharding import PartitionSpec as P

HD = 128
QBLK = 128
CHUNK = 256
TILE = 2 * QBLK
GROUP = 4
WIDE = 6
SCALE = HD ** (-0.5)
RATE = SCALE * math.log2(math.e)
FLOOR = -1e30
EXTRA = 16

smem = pl.BlockSpec(memory_space=pltpu.SMEM)
vmem = pl.BlockSpec(memory_space=pltpu.VMEM)
params = pltpu.CompilerParams(vmem_limit_bytes=32 * 1024 * 1024)
small = pltpu.CompilerParams(vmem_limit_bytes=4 * 1024 * 1024)


def dot(a, b):
    return jnp.dot(a, b, preferred_element_type=jnp.float32)


def pack_kernel(ids_ref, k_ref, q_ref, out_ref):
    rows = k_ref.shape[0]
    heads = k_ref.shape[1] // HD
    line = lax.broadcasted_iota(jnp.int32, (EXTRA, HD), 0)
    note = jnp.where(line == 0, ids_ref[0], ids_ref[1]).astype(jnp.float32).astype(out_ref.dtype)
    for slot in range(out_ref.shape[0]):
        columns = slice(slot % heads * HD, (slot % heads + 1) * HD)
        out_ref[slot, :rows, :] = k_ref[:, columns]
        out_ref[slot, rows : 2 * rows, :] = q_ref[:, columns]
        out_ref[slot, 2 * rows :, :] = note


def pack(ids, k, q, chips):
    rows = k.shape[0]
    return pl.pallas_call(
        pack_kernel,
        out_shape=jax.ShapeDtypeStruct((chips, 2 * rows + EXTRA, HD), k.dtype),
        in_specs=[smem, vmem, vmem],
        out_specs=vmem,
        name="pack",
    )(ids, k, q)


def unpack_kernel(x_ref, *out_refs):
    rows, width = out_refs[0].shape
    for i, out_ref in enumerate(out_refs):
        for head in range(width // HD):
            columns = slice(head * HD, (head + 1) * HD)
            out_ref[:, columns] = x_ref[head, i * rows : (i + 1) * rows, :]


def unpack(x, rows, heads):
    number = x.shape[1] // rows
    return pl.pallas_call(
        unpack_kernel,
        out_shape=(jax.ShapeDtypeStruct((rows, heads * HD), x.dtype),) * number,
        in_specs=[vmem],
        out_specs=(vmem,) * number,
        compiler_params=small,
        name="unpack",
    )(x)


def place_key(keys, slot, spot, k, edges):
    rows = lax.broadcasted_iota(jnp.int32, (CHUNK, HD), 0) + spot * CHUNK
    outside = (rows < edges[0:1]) | (rows >= edges[1:2])
    keys[slot, :, :HD] = k
    keys[slot, :, HD:] = jnp.where(outside, 1.0, 0.0).astype(jnp.bfloat16)


def place_query(qt, slot, q, token, sides):
    rows = slice(slot * QBLK, (slot + 1) * QBLK)
    tokens = lax.broadcasted_iota(jnp.int32, (EXTRA, QBLK), 1) + token
    within = (tokens >= sides[:EXTRA]) & (tokens < sides[EXTRA:])
    qt[:HD, rows] = q.T
    qt[HD : HD + EXTRA, rows] = jnp.where(within, FLOOR, 0.0).astype(jnp.bfloat16)


def block_rows(block, base, size):
    return pl.ds(pl.multiple_of(base + block % 2 * size, size), size)


def fetch(own, other, block, base, size):
    blocks = 2 * own.shape[0]
    here = block % blocks
    mine = own[here // 2, block_rows(here, CHUNK + base, size), :]
    theirs = other[here // 2, block_rows(here, base, size), :]
    return jnp.where(block < blocks, mine, theirs)


def prepare_kernel(
    core_ref, order_ref, units_ref, tile_ref, spot_ref, first_ref, other_ref, edges, sides,
    stats_ref,
    keys, qt, raw, tops, totals,
):
    core = core_ref[0]
    chips = first_ref.shape[0]
    tiles = stats_ref.shape[0]

    def place(i, carry):
        place_key(keys, i, 2 * i + core, first_ref[i, :CHUNK, :], edges)
        for t in (2 * i, 2 * i + 1):
            for slot in range(2):
                q = fetch(first_ref, other_ref, order_ref[2 * t + slot], 0, QBLK)
                place_query(qt.at[t], slot, q, (2 * t + slot) * QBLK, sides)
            qt[t, HD + EXTRA :, :] = jnp.zeros((HD - EXTRA, TILE), jnp.bfloat16)
            tops[t] = jnp.full((8, TILE), FLOOR, jnp.float32)
            totals[t] = jnp.zeros((8, TILE), jnp.float32)
        return carry

    lax.fori_loop(0, chips, place, 0)
    keys[chips] = jnp.ones((CHUNK, 2 * HD), jnp.bfloat16)

    def score(i, u):
        return dot(keys[spot_ref[GROUP * i + u]], qt[tile_ref[GROUP * i + u]])

    for u in range(GROUP):
        raw[0, u] = score(0, u)

    def step(i, carry):
        parts = []
        for u in range(GROUP):
            s = raw[i % 2, u].reshape(4, 8, 8, TILE)
            top = jnp.max(jnp.max(s, axis=1), axis=0)
            total = jnp.sum(jnp.sum(jnp.exp2((s - top) * RATE), axis=1), axis=0)
            parts.append((top, total))
        for u in range(GROUP):
            raw[(i + 1) % 2, u] = score(i + 1, u)
        for u, (top, total) in enumerate(parts):
            t = tile_ref[GROUP * i + u]
            old = tops[t]
            new = jnp.maximum(old, top)
            totals[t] = totals[t] * jnp.exp2((old - new) * RATE) + total * jnp.exp2((top - new) * RATE)
            tops[t] = new
        return carry

    lax.fori_loop(0, (units_ref[0] + GROUP - 1) // GROUP, step, 0)
    for t in range(tiles):
        top = tops[t]
        row_top = jnp.max(top, axis=0, keepdims=True)
        stats_ref[t, 0:1] = row_top
        stats_ref[t, 1:2] = jnp.sum(
            totals[t] * jnp.exp2((top - row_top) * RATE), axis=0, keepdims=True
        )


def prepare(scalars, first, other, edges, sides):
    chips = first.shape[0]
    tiles = 2 * chips
    pairs = tiles * TILE * 1024
    return pl.pallas_call(
        prepare_kernel,
        out_shape=jax.ShapeDtypeStruct((tiles, 2, TILE), jnp.float32),
        in_specs=[smem] * len(scalars) + [vmem] * 4,
        out_specs=vmem,
        scratch_shapes=[
            pltpu.VMEM((chips + 1, CHUNK, 2 * HD), jnp.bfloat16),
            pltpu.VMEM((tiles, 2 * HD, TILE), jnp.bfloat16),
            pltpu.VMEM((2, GROUP, CHUNK, TILE), jnp.float32),
            pltpu.VMEM((tiles, 8, TILE), jnp.float32),
            pltpu.VMEM((tiles, 8, TILE), jnp.float32),
        ],
        compiler_params=params,
        cost_estimate=pl.CostEstimate(
            flops=4 * pairs * HD, bytes_accessed=8 * 2**20, transcendentals=pairs
        ),
        name="prepare",
    )(*scalars, first, other, edges, sides)


def grads_kernel(
    core_ref, order_ref, units_ref, tile_ref, spot_ref, first_ref, other_ref, edges, sides,
    second_ref, second_other, stats_ref, stats_other,
    keep_ref, send_ref, dkv_ref,
    keys, keys_t, values, qs, qt, gs, gt, level, raw, slope, acc_k, acc_v, acc_q,
):
    core = core_ref[0]
    chips = first_ref.shape[0]

    def place(i, carry):
        k = first_ref[i, :CHUNK, :]
        place_key(keys, i, 2 * i + core, k, edges)
        keys_t[i] = k.T
        values[i, :, :HD] = second_ref[i, :CHUNK, :]
        values[i, :, HD:] = jnp.full((CHUNK, HD), -1, jnp.bfloat16)
        acc_k[i] = jnp.zeros((CHUNK, HD), jnp.float32)
        acc_v[i] = jnp.zeros((CHUNK, HD), jnp.float32)
        for t in (2 * i, 2 * i + 1):
            acc_q[t] = jnp.zeros((HD, TILE), jnp.float32)
            for slot in range(2):
                block = order_ref[2 * t + slot]
                rows = slice(slot * QBLK, (slot + 1) * QBLK)
                q = fetch(first_ref, other_ref, block, 0, QBLK)
                g = fetch(second_ref, second_other, block, 0, QBLK)
                qs[t, rows, :] = q
                gs[t, rows, :] = g
                place_query(qt.at[t], slot, q, (2 * t + slot) * QBLK, sides)
                gt[t, :HD, rows] = g.T
                gt[t, HD : HD + EXTRA, rows] = fetch(second_ref, second_other, block, CHUNK, EXTRA)
            for ref in (qt, gt):
                ref[t, HD + EXTRA :, :] = jnp.zeros((HD - EXTRA, TILE), jnp.bfloat16)
            tops = [ref[t, 0:1] for ref in (stats_ref, stats_other)]
            top = jnp.maximum(*tops)
            total = sum(
                ref[t, 1:2] * jnp.exp2((x - top) * RATE)
                for x, ref in zip(tops, (stats_ref, stats_other))
            )
            level[t] = top + jnp.log2(total) * (1.0 / RATE)
        return carry

    lax.fori_loop(0, chips, place, 0)
    keys[chips] = jnp.ones((CHUNK, 2 * HD), jnp.bfloat16)
    keys_t[chips] = jnp.zeros((HD, CHUNK), jnp.bfloat16)
    values[chips] = jnp.zeros((CHUNK, 2 * HD), jnp.bfloat16)
    acc_k[chips] = jnp.zeros((CHUNK, HD), jnp.float32)
    acc_v[chips] = jnp.zeros((CHUNK, HD), jnp.float32)

    def unit(i, u):
        return tile_ref[WIDE * i + u], spot_ref[WIDE * i + u]

    def ahead(i):
        for u in range(WIDE):
            t, spot = unit(i, u)
            raw[i % 2, u] = dot(keys[spot], qt[t])
            slope[i % 2, u] = dot(values[spot], gt[t])

    ahead(0)

    def work(i):
        for u in range(WIDE):
            t, spot = unit(i, u)
            p = jnp.exp2((raw[i % 2, u] - level[t]) * RATE)
            s = (p * slope[i % 2, u]).astype(jnp.bfloat16)
            acc_v[spot] += dot(p.astype(jnp.bfloat16), gs[t])
            acc_k[spot] += dot(s, qs[t])
            acc_q[t] += dot(keys_t[spot], s)

    def step(i, carry):
        work(i)
        ahead(i + 1)
        return carry

    last = (units_ref[0] + WIDE - 1) // WIDE - 1
    lax.fori_loop(0, last, step, 0)
    work(last)

    def hand_out(i, carry):
        dkv_ref[i, :CHUNK] = (acc_k[i] * SCALE).astype(jnp.bfloat16)
        dkv_ref[i, CHUNK:] = acc_v[i].astype(jnp.bfloat16)
        for t in (2 * i, 2 * i + 1):
            result = (acc_q[t] * SCALE).T
            for slot in range(2):
                block = order_ref[2 * t + slot]
                here = block % (2 * chips)
                rows = block_rows(here, 0, QBLK)
                part = result[slot * QBLK : (slot + 1) * QBLK]
                mine = block < 2 * chips
                keep_ref[jnp.where(mine, here // 2, chips), rows, :] = part
                send_ref[jnp.where(mine, chips, here // 2), rows, :] = part.astype(jnp.bfloat16)
        return carry

    lax.fori_loop(0, chips, hand_out, 0)


def grads(scalars, first, other, edges, sides, second, second_other, stats, stats_other):
    chips = second.shape[0]
    tiles = 2 * chips
    pairs = tiles * TILE * 1024
    bf16, f32 = jnp.bfloat16, jnp.float32
    return pl.pallas_call(
        grads_kernel,
        out_shape=(
            jax.ShapeDtypeStruct((chips + 1, TILE, HD), f32),
            jax.ShapeDtypeStruct((chips + 1, TILE, HD), bf16),
            jax.ShapeDtypeStruct((chips, 2 * CHUNK, HD), bf16),
        ),
        in_specs=[smem] * len(scalars) + [vmem] * 8,
        out_specs=(vmem,) * 3,
        scratch_shapes=[
            pltpu.VMEM((chips + 1, CHUNK, 2 * HD), bf16),
            pltpu.VMEM((chips + 1, HD, CHUNK), bf16),
            pltpu.VMEM((chips + 1, CHUNK, 2 * HD), bf16),
            pltpu.VMEM((tiles, TILE, HD), bf16),
            pltpu.VMEM((tiles, 2 * HD, TILE), bf16),
            pltpu.VMEM((tiles, TILE, HD), bf16),
            pltpu.VMEM((tiles, 2 * HD, TILE), bf16),
            pltpu.VMEM((tiles, 1, TILE), f32),
            pltpu.VMEM((2, WIDE, CHUNK, TILE), f32),
            pltpu.VMEM((2, WIDE, CHUNK, TILE), f32),
            pltpu.VMEM((chips + 1, CHUNK, HD), f32),
            pltpu.VMEM((chips + 1, CHUNK, HD), f32),
            pltpu.VMEM((tiles, HD, TILE), f32),
        ],
        compiler_params=params,
        cost_estimate=pl.CostEstimate(
            flops=10 * pairs * HD, bytes_accessed=10 * 2**20, transcendentals=pairs
        ),
        name="grads",
    )(*scalars, first, other, edges, sides, second, second_other, stats, stats_other)


def plan(lengths, core, chips):
    ends = jnp.cumsum(lengths)
    offsets = ends - lengths
    place = jnp.arange(2 * chips, dtype=jnp.int32)

    def bounds(token):
        inside = (token[:, None] >= offsets) & (token[:, None] < ends)
        return [jnp.sum(jnp.where(inside, x, 0), axis=1) for x in (offsets, ends)]

    first = bounds(place * TILE)[0] // CHUNK
    last = (bounds(place * TILE + TILE - 1)[1] - 1) // CHUNK
    chunks = 2 * jnp.arange(chips, dtype=jnp.int32) + core
    needed = (chunks[None, :] >= first[:, None]) & (chunks[None, :] <= last[:, None])
    needed = needed.astype(jnp.int32).reshape(-1)
    cells = jnp.arange(needed.shape[0], dtype=jnp.int32)
    before = jnp.sum(needed[None, :] * (cells[None, :] < cells[:, None]), axis=1)
    slots = jnp.arange(needed.shape[0] + 2 * max(GROUP, WIDE), dtype=jnp.int32)
    chosen = (before[None, :] == slots[:, None]) & (needed[None, :] > 0)
    cell = jnp.sum(jnp.where(chosen, cells[None, :], 0), axis=1)
    total = jnp.sum(needed, keepdims=True)
    spot = jnp.where(slots < total, cell % chips, chips)
    return total, cell // chips, spot


def edges_of(lengths, tokens):
    ends = jnp.cumsum(lengths)
    offsets = ends - lengths
    spare = HD - lengths.shape[0]
    edges = jnp.stack([jnp.pad(offsets, (0, spare)), jnp.pad(ends, (0, spare), constant_values=tokens)])
    spare = EXTRA - lengths.shape[0]
    sides = [jnp.pad(x, (0, spare), constant_values=tokens) for x in (offsets, ends)]
    return edges, jnp.broadcast_to(jnp.concatenate(sides)[:, None], (2 * EXTRA, QBLK))


def split_in_three(x):
    parts = []
    for _ in range(3):
        part = lax.reduce_precision(x, exponent_bits=8, mantissa_bits=7)
        parts.append(part.astype(jnp.bfloat16))
        x = x - part
    return jnp.stack(parts, axis=-2)


def on_device(queries, keys_in, values_in, forward_out, grad_out, lengths, query_block):
    size = lax.axis_size("seq")
    chips = size // 2
    core = lax.axis_index("seq") % 2
    rows = queries.shape[0]
    heads = queries.shape[1] // HD
    groups = [[2 * i + c for i in range(chips)] for c in range(2)]
    swap = [(i, i ^ 1) for i in range(size)]

    def exchange(x):
        return lax.all_to_all(x, "seq", 0, 0, axis_index_groups=groups)

    first = exchange(pack(query_block, keys_in, queries, chips))

    delta = jnp.sum(
        (grad_out.astype(jnp.float32) * forward_out.astype(jnp.float32)).reshape(rows, heads, HD),
        axis=2,
    )
    parts = split_in_three(delta.T.reshape(heads, rows // QBLK, QBLK))
    parts = jnp.pad(parts, ((0, 0), (0, 0), (0, EXTRA - 3), (0, 0))).reshape(heads, -1, HD)
    by_head = [x.reshape(rows, heads, HD).transpose(1, 0, 2) for x in (values_in, grad_out)]
    second = jnp.concatenate(by_head + [parts], axis=1)
    second = jnp.pad(second, ((0, chips - heads), (0, 0), (0, 0)))
    first, second = lax.optimization_barrier((first, second))
    second = exchange(second)

    other = lax.ppermute(first[:, rows:], "seq", swap)
    ids = jnp.concatenate([first[:, 2 * rows : 2 * rows + 2, 0], other[:, rows : rows + 2, 0]])
    ids = ids.astype(jnp.int32).reshape(-1)
    place = jnp.arange(ids.shape[0], dtype=jnp.int32)
    order = jnp.sum(jnp.where(ids[None, :] == place[:, None], place[None, :], 0), axis=1)
    units, tile, spot = plan(lengths, core, chips)
    scalars = (jnp.full((1,), core, jnp.int32), order, units, tile, spot)
    edges, sides = edges_of(lengths, size * rows)
    stats = prepare(scalars, first, other, edges, sides)
    stats_other = lax.ppermute(stats, "seq", swap)
    second, stats = lax.optimization_barrier((second, stats))
    second_other = lax.ppermute(second[:, rows:], "seq", swap)
    keep, send, dkv = grads(
        scalars, first, other, edges, sides, second, second_other, stats, stats_other
    )

    received = lax.ppermute(send, "seq", swap)
    dq = (keep + received.astype(jnp.float32))[:chips].astype(jnp.bfloat16)
    return unpack(exchange(jnp.concatenate([dq, dkv], axis=1)), rows, heads)


def solution(mesh):
    spec = P(("win", "seq"), "head")
    in_specs = (spec,) * 5 + (P("win"), P(("win", "seq")))
    return jax.shard_map(
        on_device, mesh=mesh, in_specs=in_specs, out_specs=(spec,) * 3, check_vma=False
    )
```

```python
import math

import jax
import jax.numpy as jnp
from jax import lax
from jax.experimental import pallas as pl
from jax.experimental.pallas import tpu as pltpu
from jax.sharding import PartitionSpec as P

HD = 128
QBLK = 128
CHUNK = 256
TILE = 2 * QBLK
GROUP = 6
RING = 3
SCALE = HD ** (-0.5)
RATE = SCALE * math.log2(math.e)
FLOOR = -1e30
EXTRA = 16

smem = pl.BlockSpec(memory_space=pltpu.SMEM)
vmem = pl.BlockSpec(memory_space=pltpu.VMEM)
hbm = pl.BlockSpec(memory_space=pltpu.HBM)
params = pltpu.CompilerParams(vmem_limit_bytes=32 * 1024 * 1024)
small = pltpu.CompilerParams(vmem_limit_bytes=4 * 1024 * 1024)


def dot(a, b):
    return jnp.dot(a, b, preferred_element_type=jnp.float32)


def pack_kernel(ids_ref, k_ref, q_ref, out_ref):
    rows = k_ref.shape[0]
    heads = k_ref.shape[1] // HD
    line = lax.broadcasted_iota(jnp.int32, (EXTRA, HD), 0)
    note = jnp.where(line == 0, ids_ref[0], ids_ref[1]).astype(jnp.float32).astype(out_ref.dtype)
    for slot in range(out_ref.shape[0]):
        columns = slice(slot % heads * HD, (slot % heads + 1) * HD)
        out_ref[slot, :rows, :] = k_ref[:, columns]
        out_ref[slot, rows : 2 * rows, :] = q_ref[:, columns]
        out_ref[slot, 2 * rows :, :] = note


def pack(ids, k, q, chips):
    rows = k.shape[0]
    return pl.pallas_call(
        pack_kernel,
        out_shape=jax.ShapeDtypeStruct((chips, 2 * rows + EXTRA, HD), k.dtype),
        in_specs=[smem, vmem, vmem],
        out_specs=vmem,
        name="pack",
    )(ids, k, q)


def unpack_kernel(x_ref, *out_refs):
    rows, width = out_refs[0].shape
    for i, out_ref in enumerate(out_refs):
        for head in range(width // HD):
            columns = slice(head * HD, (head + 1) * HD)
            out_ref[:, columns] = x_ref[head, i * rows : (i + 1) * rows, :]


def unpack(x, rows, heads):
    number = x.shape[1] // rows
    return pl.pallas_call(
        unpack_kernel,
        out_shape=(jax.ShapeDtypeStruct((rows, heads * HD), x.dtype),) * number,
        in_specs=[vmem],
        out_specs=(vmem,) * number,
        compiler_params=small,
        name="unpack",
    )(x)


def place_key(keys, slot, spot, k, edges):
    rows = lax.broadcasted_iota(jnp.int32, (CHUNK, HD), 0) + spot * CHUNK
    outside = (rows < edges[0:1]) | (rows >= edges[1:2])
    keys[slot, :, :HD] = k
    keys[slot, :, HD:] = jnp.where(outside, 1.0, 0.0).astype(jnp.bfloat16)


def place_query(qt, slot, q, token, sides):
    rows = slice(slot * QBLK, (slot + 1) * QBLK)
    tokens = lax.broadcasted_iota(jnp.int32, (EXTRA, QBLK), 1) + token
    within = (tokens >= sides[:EXTRA]) & (tokens < sides[EXTRA:])
    qt[:HD, rows] = q.T
    qt[HD : HD + EXTRA, rows] = jnp.where(within, FLOOR, 0.0).astype(jnp.bfloat16)


def located(order_ref, token_block, chips):
    at = order_ref[token_block]
    mine = at < 2 * chips
    here = jnp.where(mine, at, at - 2 * chips)
    return mine, lax.div(here, 2), lax.rem(here, 2)


def fetch(own, other, where, base, size):
    mine, chip, half = where
    here = own[chip, pl.ds(pl.multiple_of(CHUNK + base + half * size, size), size), :]
    there = other[chip, pl.ds(pl.multiple_of(base + half * size, size), size), :]
    return jnp.where(mine, here, there)


def looped(count, unroll, body):
    def several(i, carry):
        for j in range(unroll):
            body(unroll * i + j)
        return carry

    lax.fori_loop(0, count // unroll, several, 0)


def prepare_kernel(
    core_ref, order_ref, units_ref, tile_ref, spot_ref, first_ref, other_ref, edges, sides,
    stats_ref, scores_ref,
    keys, qt, raw, tops, totals, sems,
):
    core = core_ref[0]
    chips = first_ref.shape[0]
    tiles = stats_ref.shape[0]

    def place(i):
        place_key(keys, i, 2 * i + core, first_ref[i, :CHUNK, :], edges)
        for t in (2 * i, 2 * i + 1):
            for slot in range(2):
                where = located(order_ref, 2 * t + slot, chips)
                q = fetch(first_ref, other_ref, where, 0, QBLK)
                place_query(qt.at[t], slot, q, (2 * t + slot) * QBLK, sides)
            qt[t, HD + EXTRA :, :] = jnp.zeros((HD - EXTRA, TILE), jnp.bfloat16)
            tops[t] = jnp.full((8, TILE), FLOOR, jnp.float32)
            totals[t] = jnp.zeros((8, TILE), jnp.float32)

    looped(chips, 2, place)
    keys[chips] = jnp.ones((CHUNK, 2 * HD), jnp.bfloat16)

    def score(i, u):
        return dot(keys[spot_ref[GROUP * i + u]], qt[tile_ref[GROUP * i + u]])

    for u in range(GROUP):
        raw[0, u] = score(0, u)

    def hand_over(i):
        slot = i % RING
        return pltpu.make_async_copy(raw.at[slot], scores_ref.at[i], sems.at[slot])

    steps = (units_ref[0] + GROUP - 1) // GROUP

    def step(i, carry):
        @pl.when(i >= RING - 1)
        def _():
            hand_over(i - (RING - 1)).wait()

        hand_over(i).start()
        parts = []
        for u in range(GROUP):
            s = raw[i % RING, u].reshape(4, 8, 8, TILE)
            top = jnp.max(jnp.max(s, axis=1), axis=0)
            total = jnp.sum(jnp.sum(jnp.exp2((s - top) * RATE), axis=1), axis=0)
            parts.append((top, total))
        for u in range(GROUP):
            raw[(i + 1) % RING, u] = score(i + 1, u)
        for u, (top, total) in enumerate(parts):
            t = tile_ref[GROUP * i + u]
            old = tops[t]
            new = jnp.maximum(old, top)
            totals[t] = totals[t] * jnp.exp2((old - new) * RATE) + total * jnp.exp2((top - new) * RATE)
            tops[t] = new
        return carry

    lax.fori_loop(0, steps, step, 0)
    for t in range(tiles):
        top = tops[t]
        row_top = jnp.max(top, axis=0, keepdims=True)
        stats_ref[t, 0:1] = row_top
        stats_ref[t, 1:2] = jnp.sum(
            totals[t] * jnp.exp2((top - row_top) * RATE), axis=0, keepdims=True
        )
    for back in range(RING - 1, 0, -1):
        @pl.when(steps >= back)
        def _():
            hand_over(steps - back).wait()


def prepare(scalars, first, other, edges, sides):
    chips = first.shape[0]
    tiles = 2 * chips
    pairs = tiles * TILE * 1024
    steps = (tiles * chips + GROUP - 1) // GROUP
    return pl.pallas_call(
        prepare_kernel,
        out_shape=(
            jax.ShapeDtypeStruct((tiles, 2, TILE), jnp.float32),
            jax.ShapeDtypeStruct((steps, GROUP, CHUNK, TILE), jnp.float32),
        ),
        in_specs=[smem] * len(scalars) + [vmem] * 4,
        out_specs=(vmem, hbm),
        scratch_shapes=[
            pltpu.VMEM((chips + 1, CHUNK, 2 * HD), jnp.bfloat16),
            pltpu.VMEM((tiles, 2 * HD, TILE), jnp.bfloat16),
            pltpu.VMEM((RING, GROUP, CHUNK, TILE), jnp.float32),
            pltpu.VMEM((tiles, 8, TILE), jnp.float32),
            pltpu.VMEM((tiles, 8, TILE), jnp.float32),
            pltpu.SemaphoreType.DMA((RING,)),
        ],
        compiler_params=params,
        cost_estimate=pl.CostEstimate(
            flops=4 * pairs * HD, bytes_accessed=8 * 2**20, transcendentals=pairs
        ),
        name="prepare",
    )(*scalars, first, other, edges, sides)


def grads_kernel(
    core_ref, order_ref, units_ref, tile_ref, spot_ref, first_ref, other_ref,
    second_ref, second_other, stats_ref, stats_other, scores_ref,
    keep_ref, send_ref, dkv_ref,
    keys_t, values, qs, gs, gt, level, raw, slope, acc_k, acc_v, acc_q, sems,
):
    chips = first_ref.shape[0]
    steps = (units_ref[0] + GROUP - 1) // GROUP

    def take_over(i):
        slot = i % RING
        return [
            pltpu.make_async_copy(scores_ref.at[i, u], raw.at[slot, u], sems.at[slot, u])
            for u in range(GROUP)
        ]

    def begin(i):
        @pl.when(i < steps)
        def _():
            for copy in take_over(i):
                copy.start()

    for i in range(RING - 1):
        begin(i)

    def place(i):
        keys_t[i] = first_ref[i, :CHUNK, :].T
        values[i, :, :HD] = second_ref[i, :CHUNK, :]
        values[i, :, HD:] = jnp.full((CHUNK, HD), -1, jnp.bfloat16)
        acc_k[i] = jnp.zeros((CHUNK, HD), jnp.float32)
        acc_v[i] = jnp.zeros((CHUNK, HD), jnp.float32)
        for t in (2 * i, 2 * i + 1):
            acc_q[t] = jnp.zeros((HD, TILE), jnp.float32)
            for slot in range(2):
                rows = slice(slot * QBLK, (slot + 1) * QBLK)
                where = located(order_ref, 2 * t + slot, chips)
                q = fetch(first_ref, other_ref, where, 0, QBLK)
                g = fetch(second_ref, second_other, where, 0, QBLK)
                qs[t, rows, :] = q
                gs[t, rows, :] = g
                gt[t, :HD, rows] = g.T
                delta = fetch(second_ref, second_other, where, CHUNK, EXTRA)
                gt[t, HD : HD + EXTRA, rows] = delta
            gt[t, HD + EXTRA :, :] = jnp.zeros((HD - EXTRA, TILE), jnp.bfloat16)
            tops = [ref[t, 0:1] for ref in (stats_ref, stats_other)]
            top = jnp.maximum(*tops)
            total = sum(
                ref[t, 1:2] * jnp.exp2((x - top) * RATE)
                for x, ref in zip(tops, (stats_ref, stats_other))
            )
            level[t] = top + jnp.log2(total) * (1.0 / RATE)

    looped(chips, 2, place)
    keys_t[chips] = jnp.zeros((HD, CHUNK), jnp.bfloat16)
    values[chips] = jnp.zeros((CHUNK, 2 * HD), jnp.bfloat16)
    acc_k[chips] = jnp.zeros((CHUNK, HD), jnp.float32)
    acc_v[chips] = jnp.zeros((CHUNK, HD), jnp.float32)

    def unit(i, u):
        return tile_ref[GROUP * i + u], spot_ref[GROUP * i + u]

    def ahead(i):
        for u in range(GROUP):
            t, spot = unit(i, u)
            slope[i % 2, u] = dot(values[spot], gt[t])

    ahead(0)

    def work(i):
        for copy in take_over(i):
            copy.wait()
        begin(i + RING - 1)
        for u in range(GROUP):
            t, spot = unit(i, u)
            p = jnp.exp2((raw[i % RING, u] - level[t]) * RATE)
            s = (p * slope[i % 2, u]).astype(jnp.bfloat16)
            acc_v[spot] += dot(p.astype(jnp.bfloat16), gs[t])
            acc_k[spot] += dot(s, qs[t])
            acc_q[t] += dot(keys_t[spot], s)

    def step(i, carry):
        work(i)
        ahead(i + 1)
        return carry

    lax.fori_loop(0, steps - 1, step, 0)
    work(steps - 1)

    def hand_out(i):
        dkv_ref[i, :CHUNK] = (acc_k[i] * SCALE).astype(jnp.bfloat16)
        dkv_ref[i, CHUNK:] = acc_v[i].astype(jnp.bfloat16)
        for t in (2 * i, 2 * i + 1):
            result = (acc_q[t] * SCALE).T
            for slot in range(2):
                mine, chip, half = located(order_ref, 2 * t + slot, chips)
                rows = pl.ds(pl.multiple_of(half * QBLK, QBLK), QBLK)
                part = result[slot * QBLK : (slot + 1) * QBLK]
                keep_ref[jnp.where(mine, chip, chips), rows, :] = part
                send_ref[jnp.where(mine, chips, chip), rows, :] = part.astype(jnp.bfloat16)

    looped(chips, 2, hand_out)


def grads(scalars, first, other, second, second_other, stats, stats_other, scores):
    chips = second.shape[0]
    tiles = 2 * chips
    pairs = tiles * TILE * 1024
    bf16, f32 = jnp.bfloat16, jnp.float32
    return pl.pallas_call(
        grads_kernel,
        out_shape=(
            jax.ShapeDtypeStruct((chips + 1, TILE, HD), f32),
            jax.ShapeDtypeStruct((chips + 1, TILE, HD), bf16),
            jax.ShapeDtypeStruct((chips, 2 * CHUNK, HD), bf16),
        ),
        in_specs=[smem] * len(scalars) + [vmem] * 6 + [hbm],
        out_specs=(vmem,) * 3,
        scratch_shapes=[
            pltpu.VMEM((chips + 1, HD, CHUNK), bf16),
            pltpu.VMEM((chips + 1, CHUNK, 2 * HD), bf16),
            pltpu.VMEM((tiles, TILE, HD), bf16),
            pltpu.VMEM((tiles, TILE, HD), bf16),
            pltpu.VMEM((tiles, 2 * HD, TILE), bf16),
            pltpu.VMEM((tiles, 1, TILE), f32),
            pltpu.VMEM((RING, GROUP, CHUNK, TILE), f32),
            pltpu.VMEM((2, GROUP, CHUNK, TILE), f32),
            pltpu.VMEM((chips + 1, CHUNK, HD), f32),
            pltpu.VMEM((chips + 1, CHUNK, HD), f32),
            pltpu.VMEM((tiles, HD, TILE), f32),
            pltpu.SemaphoreType.DMA((RING, GROUP)),
        ],
        compiler_params=params,
        cost_estimate=pl.CostEstimate(
            flops=10 * pairs * HD, bytes_accessed=10 * 2**20, transcendentals=pairs
        ),
        name="grads",
    )(*scalars, first, other, second, second_other, stats, stats_other, scores)


def plan(lengths, core, chips):
    ends = jnp.cumsum(lengths)
    offsets = ends - lengths
    place = jnp.arange(2 * chips, dtype=jnp.int32)

    def bounds(token):
        inside = (token[:, None] >= offsets) & (token[:, None] < ends)
        return [jnp.sum(jnp.where(inside, x, 0), axis=1) for x in (offsets, ends)]

    first = bounds(place * TILE)[0] // CHUNK
    last = (bounds(place * TILE + TILE - 1)[1] - 1) // CHUNK
    chunks = 2 * jnp.arange(chips, dtype=jnp.int32) + core
    needed = (chunks[None, :] >= first[:, None]) & (chunks[None, :] <= last[:, None])
    needed = needed.astype(jnp.int32).reshape(-1)
    cells = jnp.arange(needed.shape[0], dtype=jnp.int32)
    before = jnp.sum(needed[None, :] * (cells[None, :] < cells[:, None]), axis=1)
    slots = jnp.arange(needed.shape[0] + 2 * GROUP, dtype=jnp.int32)
    chosen = (before[None, :] == slots[:, None]) & (needed[None, :] > 0)
    cell = jnp.sum(jnp.where(chosen, cells[None, :], 0), axis=1)
    total = jnp.sum(needed, keepdims=True)
    spot = jnp.where(slots < total, cell % chips, chips)
    return total, cell // chips, spot


def edges_of(lengths, tokens):
    ends = jnp.cumsum(lengths)
    offsets = ends - lengths
    spare = HD - lengths.shape[0]
    edges = jnp.stack([jnp.pad(offsets, (0, spare)), jnp.pad(ends, (0, spare), constant_values=tokens)])
    spare = EXTRA - lengths.shape[0]
    sides = [jnp.pad(x, (0, spare), constant_values=tokens) for x in (offsets, ends)]
    return edges, jnp.broadcast_to(jnp.concatenate(sides)[:, None], (2 * EXTRA, QBLK))


def split_in_three(x):
    parts = []
    for _ in range(3):
        part = lax.reduce_precision(x, exponent_bits=8, mantissa_bits=7)
        parts.append(part.astype(jnp.bfloat16))
        x = x - part
    return jnp.stack(parts, axis=-2)


def on_device(queries, keys_in, values_in, forward_out, grad_out, lengths, query_block):
    size = lax.axis_size("seq")
    chips = size // 2
    core = lax.axis_index("seq") % 2
    rows = queries.shape[0]
    heads = queries.shape[1] // HD
    groups = [[2 * i + c for i in range(chips)] for c in range(2)]
    swap = [(i, i ^ 1) for i in range(size)]

    def exchange(x):
        return lax.all_to_all(x, "seq", 0, 0, axis_index_groups=groups)

    first = exchange(pack(query_block, keys_in, queries, chips))

    delta = jnp.sum(
        (grad_out.astype(jnp.float32) * forward_out.astype(jnp.float32)).reshape(rows, heads, HD),
        axis=2,
    )
    parts = split_in_three(delta.T.reshape(heads, rows // QBLK, QBLK))
    parts = jnp.pad(parts, ((0, 0), (0, 0), (0, EXTRA - 3), (0, 0))).reshape(heads, -1, HD)
    by_head = [x.reshape(rows, heads, HD).transpose(1, 0, 2) for x in (values_in, grad_out)]
    second = jnp.concatenate(by_head + [parts], axis=1)
    second = jnp.pad(second, ((0, chips - heads), (0, 0), (0, 0)))
    first, second = lax.optimization_barrier((first, second))
    second = exchange(second)

    other = lax.ppermute(first[:, rows:], "seq", swap)
    ids = jnp.concatenate([first[:, 2 * rows : 2 * rows + 2, 0], other[:, rows : rows + 2, 0]])
    ids = ids.astype(jnp.int32).reshape(-1)
    place = jnp.arange(ids.shape[0], dtype=jnp.int32)
    order = jnp.sum(jnp.where(ids[None, :] == place[:, None], place[None, :], 0), axis=1)
    units, tile, spot = plan(lengths, core, chips)
    scalars = (jnp.full((1,), core, jnp.int32), order, units, tile, spot)
    edges, sides = edges_of(lengths, size * rows)
    stats, scores = prepare(scalars, first, other, edges, sides)
    stats_other = lax.ppermute(stats, "seq", swap)
    second, stats = lax.optimization_barrier((second, stats))
    second_other = lax.ppermute(second[:, rows:], "seq", swap)
    keep, send, dkv = grads(
        scalars, first, other, second, second_other, stats, stats_other, scores
    )

    received = lax.ppermute(send, "seq", swap)
    dq = (keep + received.astype(jnp.float32))[:chips].astype(jnp.bfloat16)
    return unpack(exchange(jnp.concatenate([dq, dkv], axis=1)), rows, heads)


def solution(mesh):
    spec = P(("win", "seq"), "head")
    in_specs = (spec,) * 5 + (P("win"), P(("win", "seq")))
    return jax.shard_map(
        on_device, mesh=mesh, in_specs=in_specs, out_specs=(spec,) * 3, check_vma=False
    )
```

```python
import math

import jax
import jax.numpy as jnp
from jax import lax
from jax.experimental import pallas as pl
from jax.experimental.pallas import tpu as pltpu
from jax.sharding import PartitionSpec as P

HD = 128
QBLK = 128
CHUNK = 256
TILE = 2 * QBLK
GROUP = 6
RING = 3
SCALE = HD ** (-0.5)
RATE = SCALE * math.log2(math.e)
FLOOR = -1e30
EXTRA = 16

smem = pl.BlockSpec(memory_space=pltpu.SMEM)
vmem = pl.BlockSpec(memory_space=pltpu.VMEM)
hbm = pl.BlockSpec(memory_space=pltpu.HBM)
params = pltpu.CompilerParams(vmem_limit_bytes=32 * 1024 * 1024)
small = pltpu.CompilerParams(vmem_limit_bytes=4 * 1024 * 1024)


def dot(a, b):
    return jnp.dot(a, b, preferred_element_type=jnp.float32)


def pack_kernel(ids_ref, k_ref, q_ref, out_ref):
    rows = k_ref.shape[0]
    heads = k_ref.shape[1] // HD
    line = lax.broadcasted_iota(jnp.int32, (EXTRA, HD), 0)
    note = jnp.where(line == 0, ids_ref[0], ids_ref[1]).astype(jnp.float32).astype(out_ref.dtype)
    for slot in range(out_ref.shape[0]):
        columns = slice(slot % heads * HD, (slot % heads + 1) * HD)
        out_ref[slot, :rows, :] = k_ref[:, columns]
        out_ref[slot, rows : 2 * rows, :] = q_ref[:, columns]
        out_ref[slot, 2 * rows :, :] = note


def pack(ids, k, q, chips):
    rows = k.shape[0]
    return pl.pallas_call(
        pack_kernel,
        out_shape=jax.ShapeDtypeStruct((chips, 2 * rows + EXTRA, HD), k.dtype),
        in_specs=[smem, vmem, vmem],
        out_specs=vmem,
        name="pack",
    )(ids, k, q)


def unpack_kernel(x_ref, *out_refs):
    rows, width = out_refs[0].shape
    for i, out_ref in enumerate(out_refs):
        for head in range(width // HD):
            columns = slice(head * HD, (head + 1) * HD)
            out_ref[:, columns] = x_ref[head, i * rows : (i + 1) * rows, :]


def unpack(x, rows, heads):
    number = x.shape[1] // rows
    return pl.pallas_call(
        unpack_kernel,
        out_shape=(jax.ShapeDtypeStruct((rows, heads * HD), x.dtype),) * number,
        in_specs=[vmem],
        out_specs=(vmem,) * number,
        compiler_params=small,
        name="unpack",
    )(x)


def place_key(keys, slot, spot, k, edges):
    rows = lax.broadcasted_iota(jnp.int32, (CHUNK, HD), 0) + spot * CHUNK
    outside = (rows < edges[0:1]) | (rows >= edges[1:2])
    keys[slot, :, :HD] = k
    keys[slot, :, HD:] = jnp.where(outside, 1.0, 0.0).astype(jnp.bfloat16)


def place_query(qt, slot, q, token, sides):
    rows = slice(slot * QBLK, (slot + 1) * QBLK)
    tokens = lax.broadcasted_iota(jnp.int32, (EXTRA, QBLK), 1) + token
    within = (tokens >= sides[:EXTRA]) & (tokens < sides[EXTRA:])
    qt[:HD, rows] = q.T
    qt[HD : HD + EXTRA, rows] = jnp.where(within, FLOOR, 0.0).astype(jnp.bfloat16)


def located(order_ref, token_block, chips):
    at = order_ref[token_block]
    mine = at < 2 * chips
    here = jnp.where(mine, at, at - 2 * chips)
    return mine, lax.div(here, 2), lax.rem(here, 2)


def fetch(own, other, where, base, size):
    mine, chip, half = where
    here = own[chip, pl.ds(pl.multiple_of(CHUNK + base + half * size, size), size), :]
    there = other[chip, pl.ds(pl.multiple_of(base + half * size, size), size), :]
    return jnp.where(mine, here, there)


def looped(count, unroll, body):
    def several(i, carry):
        for j in range(unroll):
            body(unroll * i + j)
        return carry

    lax.fori_loop(0, count // unroll, several, 0)


def prepare_kernel(
    core_ref, order_ref, units_ref, tile_ref, spot_ref, first_ref, other_ref, edges, sides,
    stats_ref, scores_ref,
    keys, qt, raw, tops, totals, sems,
):
    core = core_ref[0]
    chips = first_ref.shape[0]
    tiles = stats_ref.shape[0]

    def place(i):
        place_key(keys, i, 2 * i + core, first_ref[i, :CHUNK, :], edges)
        for t in (2 * i, 2 * i + 1):
            for slot in range(2):
                where = located(order_ref, 2 * t + slot, chips)
                q = fetch(first_ref, other_ref, where, 0, QBLK)
                place_query(qt.at[t], slot, q, (2 * t + slot) * QBLK, sides)
            qt[t, HD + EXTRA :, :] = jnp.zeros((HD - EXTRA, TILE), jnp.bfloat16)
            tops[t] = jnp.full((8, TILE), FLOOR, jnp.float32)
            totals[t] = jnp.zeros((8, TILE), jnp.float32)

    looped(chips, 4, place)
    keys[chips] = jnp.ones((CHUNK, 2 * HD), jnp.bfloat16)

    def score(i, u):
        return dot(keys[spot_ref[GROUP * i + u]], qt[tile_ref[GROUP * i + u]])

    for u in range(GROUP):
        raw[0, u] = score(0, u)

    def hand_over(i):
        slot = i % RING
        return pltpu.make_async_copy(raw.at[slot], scores_ref.at[i], sems.at[slot])

    steps = (units_ref[0] + GROUP - 1) // GROUP

    def step(i, carry):
        @pl.when(i >= RING - 1)
        def _():
            hand_over(i - (RING - 1)).wait()

        hand_over(i).start()
        parts = []
        for u in range(GROUP):
            s = raw[i % RING, u].reshape(4, 8, 8, TILE)
            top = jnp.max(jnp.max(s, axis=1), axis=0)
            total = jnp.sum(jnp.sum(jnp.exp2((s - top) * RATE), axis=1), axis=0)
            parts.append((top, total))
        for u in range(GROUP):
            raw[(i + 1) % RING, u] = score(i + 1, u)
        for u, (top, total) in enumerate(parts):
            t = tile_ref[GROUP * i + u]
            old = tops[t]
            new = jnp.maximum(old, top)
            totals[t] = totals[t] * jnp.exp2((old - new) * RATE) + total * jnp.exp2((top - new) * RATE)
            tops[t] = new
        return carry

    lax.fori_loop(0, steps, step, 0)
    for t in range(tiles):
        top = tops[t]
        row_top = jnp.max(top, axis=0, keepdims=True)
        stats_ref[t, 0:1] = row_top
        stats_ref[t, 1:2] = jnp.sum(
            totals[t] * jnp.exp2((top - row_top) * RATE), axis=0, keepdims=True
        )
    for back in range(RING - 1, 0, -1):
        @pl.when(steps >= back)
        def _():
            hand_over(steps - back).wait()


def prepare(scalars, first, other, edges, sides):
    chips = first.shape[0]
    tiles = 2 * chips
    pairs = tiles * TILE * 1024
    steps = (tiles * chips + GROUP - 1) // GROUP
    return pl.pallas_call(
        prepare_kernel,
        out_shape=(
            jax.ShapeDtypeStruct((tiles, 2, TILE), jnp.float32),
            jax.ShapeDtypeStruct((steps, GROUP, CHUNK, TILE), jnp.float32),
        ),
        in_specs=[smem] * len(scalars) + [vmem] * 4,
        out_specs=(vmem, hbm),
        scratch_shapes=[
            pltpu.VMEM((chips + 1, CHUNK, 2 * HD), jnp.bfloat16),
            pltpu.VMEM((tiles, 2 * HD, TILE), jnp.bfloat16),
            pltpu.VMEM((RING, GROUP, CHUNK, TILE), jnp.float32),
            pltpu.VMEM((tiles, 8, TILE), jnp.float32),
            pltpu.VMEM((tiles, 8, TILE), jnp.float32),
            pltpu.SemaphoreType.DMA((RING,)),
        ],
        compiler_params=params,
        cost_estimate=pl.CostEstimate(
            flops=4 * pairs * HD, bytes_accessed=8 * 2**20, transcendentals=pairs
        ),
        name="prepare",
    )(*scalars, first, other, edges, sides)


def grads_kernel(
    core_ref, order_ref, units_ref, tile_ref, spot_ref, first_ref, other_ref,
    second_ref, second_other, stats_ref, stats_other, scores_ref,
    keep_ref, send_ref, dkv_ref,
    keys_t, values, qs, gs, gt, level, raw, acc_k, acc_v, acc_q, sems,
):
    chips = first_ref.shape[0]
    steps = (units_ref[0] + GROUP - 1) // GROUP

    def take_over(i):
        slot = i % RING
        return [
            pltpu.make_async_copy(scores_ref.at[i, u], raw.at[slot, u], sems.at[slot, u])
            for u in range(GROUP)
        ]

    def begin(i):
        @pl.when(i < steps)
        def _():
            for copy in take_over(i):
                copy.start()

    for i in range(RING - 1):
        begin(i)

    def place(i):
        keys_t[i] = first_ref[i, :CHUNK, :].T
        values[i, :, :HD] = second_ref[i, :CHUNK, :]
        values[i, :, HD:] = jnp.full((CHUNK, HD), -1, jnp.bfloat16)
        acc_k[i] = jnp.zeros((CHUNK, HD), jnp.float32)
        acc_v[i] = jnp.zeros((CHUNK, HD), jnp.float32)
        for t in (2 * i, 2 * i + 1):
            acc_q[t] = jnp.zeros((HD, TILE), jnp.float32)
            for slot in range(2):
                rows = slice(slot * QBLK, (slot + 1) * QBLK)
                where = located(order_ref, 2 * t + slot, chips)
                q = fetch(first_ref, other_ref, where, 0, QBLK)
                g = fetch(second_ref, second_other, where, 0, QBLK)
                qs[t, rows, :] = q
                gs[t, rows, :] = g
                gt[t, :HD, rows] = g.T
                delta = fetch(second_ref, second_other, where, CHUNK, EXTRA)
                gt[t, HD : HD + EXTRA, rows] = delta
            gt[t, HD + EXTRA :, :] = jnp.zeros((HD - EXTRA, TILE), jnp.bfloat16)
            tops = [ref[t, 0:1] for ref in (stats_ref, stats_other)]
            top = jnp.maximum(*tops)
            total = sum(
                ref[t, 1:2] * jnp.exp2((x - top) * RATE)
                for x, ref in zip(tops, (stats_ref, stats_other))
            )
            level[t] = top + jnp.log2(total) * (1.0 / RATE)

    looped(chips, 4, place)
    keys_t[chips] = jnp.zeros((HD, CHUNK), jnp.bfloat16)
    values[chips] = jnp.zeros((CHUNK, 2 * HD), jnp.bfloat16)
    acc_k[chips] = jnp.zeros((CHUNK, HD), jnp.float32)
    acc_v[chips] = jnp.zeros((CHUNK, HD), jnp.float32)

    def unit(i, u):
        return tile_ref[GROUP * i + u], spot_ref[GROUP * i + u]

    def work(i):
        for copy in take_over(i):
            copy.wait()
        begin(i + RING - 1)
        units = [unit(i, u) for u in range(GROUP)]
        slopes = {}
        lows = {}

        def slope(u):
            if u < GROUP:
                t, spot = units[u]
                slopes[u] = dot(values[spot], gt[t])

        def finish(u):
            if 0 <= u < GROUP:
                t, spot = units[u]
                acc_k[spot] += dot(lows[u], qs[t])
                acc_q[t] += dot(keys_t[spot], lows[u])

        for u in range(2):
            slope(u)
        for u, (t, spot) in enumerate(units):
            p = jnp.exp2((raw[i % RING, u] - level[t]) * RATE)
            slope(u + 2)
            acc_v[spot] += dot(p.astype(jnp.bfloat16), gs[t])
            lows[u] = (p * slopes[u]).astype(jnp.bfloat16)
            finish(u - 1)
        for u in range(GROUP - 1, GROUP):
            finish(u)

    def step(i, carry):
        work(i)
        return carry

    lax.fori_loop(0, steps, step, 0)

    def hand_out(i):
        dkv_ref[i, :CHUNK] = (acc_k[i] * SCALE).astype(jnp.bfloat16)
        dkv_ref[i, CHUNK:] = acc_v[i].astype(jnp.bfloat16)
        for t in (2 * i, 2 * i + 1):
            result = (acc_q[t] * SCALE).T
            for slot in range(2):
                mine, chip, half = located(order_ref, 2 * t + slot, chips)
                rows = pl.ds(pl.multiple_of(half * QBLK, QBLK), QBLK)
                part = result[slot * QBLK : (slot + 1) * QBLK]
                keep_ref[jnp.where(mine, chip, chips), rows, :] = part
                send_ref[jnp.where(mine, chips, chip), rows, :] = part.astype(jnp.bfloat16)

    looped(chips, 4, hand_out)


def grads(scalars, first, other, second, second_other, stats, stats_other, scores):
    chips = second.shape[0]
    tiles = 2 * chips
    pairs = tiles * TILE * 1024
    bf16, f32 = jnp.bfloat16, jnp.float32
    return pl.pallas_call(
        grads_kernel,
        out_shape=(
            jax.ShapeDtypeStruct((chips + 1, TILE, HD), f32),
            jax.ShapeDtypeStruct((chips + 1, TILE, HD), bf16),
            jax.ShapeDtypeStruct((chips, 2 * CHUNK, HD), bf16),
        ),
        in_specs=[smem] * len(scalars) + [vmem] * 6 + [hbm],
        out_specs=(vmem,) * 3,
        scratch_shapes=[
            pltpu.VMEM((chips + 1, HD, CHUNK), bf16),
            pltpu.VMEM((chips + 1, CHUNK, 2 * HD), bf16),
            pltpu.VMEM((tiles, TILE, HD), bf16),
            pltpu.VMEM((tiles, TILE, HD), bf16),
            pltpu.VMEM((tiles, 2 * HD, TILE), bf16),
            pltpu.VMEM((tiles, 1, TILE), f32),
            pltpu.VMEM((RING, GROUP, CHUNK, TILE), f32),
            pltpu.VMEM((chips + 1, CHUNK, HD), f32),
            pltpu.VMEM((chips + 1, CHUNK, HD), f32),
            pltpu.VMEM((tiles, HD, TILE), f32),
            pltpu.SemaphoreType.DMA((RING, GROUP)),
        ],
        compiler_params=params,
        cost_estimate=pl.CostEstimate(
            flops=10 * pairs * HD, bytes_accessed=10 * 2**20, transcendentals=pairs
        ),
        name="grads",
    )(*scalars, first, other, second, second_other, stats, stats_other, scores)


def plan(lengths, core, chips):
    ends = jnp.cumsum(lengths)
    offsets = ends - lengths
    place = jnp.arange(2 * chips, dtype=jnp.int32)

    def bounds(token):
        inside = (token[:, None] >= offsets) & (token[:, None] < ends)
        return [jnp.sum(jnp.where(inside, x, 0), axis=1) for x in (offsets, ends)]

    first = bounds(place * TILE)[0] // CHUNK
    last = (bounds(place * TILE + TILE - 1)[1] - 1) // CHUNK
    chunks = 2 * jnp.arange(chips, dtype=jnp.int32) + core
    needed = (chunks[None, :] >= first[:, None]) & (chunks[None, :] <= last[:, None])
    needed = needed.astype(jnp.int32).reshape(-1)
    cells = jnp.arange(needed.shape[0], dtype=jnp.int32)
    before = jnp.sum(needed[None, :] * (cells[None, :] < cells[:, None]), axis=1)
    slots = jnp.arange(needed.shape[0] + 2 * GROUP, dtype=jnp.int32)
    chosen = (before[None, :] == slots[:, None]) & (needed[None, :] > 0)
    cell = jnp.sum(jnp.where(chosen, cells[None, :], 0), axis=1)
    total = jnp.sum(needed, keepdims=True)
    spot = jnp.where(slots < total, cell % chips, chips)
    return total, cell // chips, spot


def edges_of(lengths, tokens):
    ends = jnp.cumsum(lengths)
    offsets = ends - lengths
    spare = HD - lengths.shape[0]
    edges = jnp.stack([jnp.pad(offsets, (0, spare)), jnp.pad(ends, (0, spare), constant_values=tokens)])
    spare = EXTRA - lengths.shape[0]
    sides = [jnp.pad(x, (0, spare), constant_values=tokens) for x in (offsets, ends)]
    return edges, jnp.broadcast_to(jnp.concatenate(sides)[:, None], (2 * EXTRA, QBLK))


def split_in_three(x):
    parts = []
    for _ in range(3):
        part = lax.reduce_precision(x, exponent_bits=8, mantissa_bits=7)
        parts.append(part.astype(jnp.bfloat16))
        x = x - part
    return jnp.stack(parts, axis=-2)


def on_device(queries, keys_in, values_in, forward_out, grad_out, lengths, query_block):
    size = lax.axis_size("seq")
    chips = size // 2
    core = lax.axis_index("seq") % 2
    rows = queries.shape[0]
    heads = queries.shape[1] // HD
    groups = [[2 * i + c for i in range(chips)] for c in range(2)]
    swap = [(i, i ^ 1) for i in range(size)]

    def exchange(x):
        return lax.all_to_all(x, "seq", 0, 0, axis_index_groups=groups)

    first = exchange(pack(query_block, keys_in, queries, chips))

    delta = jnp.sum(
        (grad_out.astype(jnp.float32) * forward_out.astype(jnp.float32)).reshape(rows, heads, HD),
        axis=2,
    )
    parts = split_in_three(delta.T.reshape(heads, rows // QBLK, QBLK))
    parts = jnp.pad(parts, ((0, 0), (0, 0), (0, EXTRA - 3), (0, 0))).reshape(heads, -1, HD)
    by_head = [x.reshape(rows, heads, HD).transpose(1, 0, 2) for x in (values_in, grad_out)]
    second = jnp.concatenate(by_head + [parts], axis=1)
    second = jnp.pad(second, ((0, chips - heads), (0, 0), (0, 0)))
    first, second = lax.optimization_barrier((first, second))
    second = exchange(second)

    other = lax.ppermute(first[:, rows:], "seq", swap)
    ids = jnp.concatenate([first[:, 2 * rows : 2 * rows + 2, 0], other[:, rows : rows + 2, 0]])
    ids = ids.astype(jnp.int32).reshape(-1)
    place = jnp.arange(ids.shape[0], dtype=jnp.int32)
    order = jnp.sum(jnp.where(ids[None, :] == place[:, None], place[None, :], 0), axis=1)
    units, tile, spot = plan(lengths, core, chips)
    scalars = (jnp.full((1,), core, jnp.int32), order, units, tile, spot)
    edges, sides = edges_of(lengths, size * rows)
    stats, scores = prepare(scalars, first, other, edges, sides)
    stats_other = lax.ppermute(stats, "seq", swap)
    second, stats = lax.optimization_barrier((second, stats))
    second_other = lax.ppermute(second[:, rows:], "seq", swap)
    keep, send, dkv = grads(
        scalars, first, other, second, second_other, stats, stats_other, scores
    )

    received = lax.ppermute(send, "seq", swap)
    dq = (keep + received.astype(jnp.float32))[:chips].astype(jnp.bfloat16)
    return unpack(exchange(jnp.concatenate([dq, dkv], axis=1)), rows, heads)


def solution(mesh):
    spec = P(("win", "seq"), "head")
    in_specs = (spec,) * 5 + (P("win"), P(("win", "seq")))
    return jax.shard_map(
        on_device, mesh=mesh, in_specs=in_specs, out_specs=(spec,) * 3, check_vma=False
    )
```
